256 devices in a mesh: row: 16 (over y, x), col: 16 (over z, core).
Axes of the slice: x: 4, y: 4, z: 8, core: 2. Of those that a mesh axis runs over, the one named last changes fastest.
Arguments:
- matrix: float32 [20480, 20480], P('row', 'col'), as said below
Outputs:
- factored: float32 [20480, 20480], P('row', 'col')
Inputs may be any that keep to these rules, and one draw needn't show every extreme that they name: `matrix`: symmetric positive definite in global order, stored in the tile storage of the statement.
All inputs are finite; a program needn't handle non-finite values.
Results may differ from the reference program's by a relative error of at most 0.000053.
Values sent between devices are 32-bit elements; how exact they have to be, the bound alone decides.
A program may use at most 128 MiB of HBM per device.

```python
import jax
import jax.numpy as jnp
from jax import lax

TILE = 128
TILES = 160
ORDER = 20480
N_ROW = 16
N_COL = 16


def to_stored_draw(whole):
    rows_tiles = TILES // N_ROW
    cols_tiles = TILES // N_COL
    shaped = whole.reshape(rows_tiles, N_ROW, TILE, cols_tiles, N_COL, TILE)
    return shaped.transpose(1, 0, 2, 4, 3, 5).reshape(ORDER, ORDER)


def stokeslet_blocks(px_pos, py_pos, pz_pos, radius):
    delta_x = px_pos[:, None] - px_pos[None, :]
    delta_y = py_pos[:, None] - py_pos[None, :]
    delta_z = pz_pos[:, None] - pz_pos[None, :]
    dist_sq = delta_x * delta_x + delta_y * delta_y + delta_z * delta_z
    soft = dist_sq + radius
    factor = 0.5 / (soft * jnp.sqrt(soft))
    isotropic = (dist_sq + 2.0) * factor
    parts = (delta_x, delta_y, delta_z)
    rows_list = []
    for first in range(3):
        entries = []
        for second in range(3):
            entry = parts[first] * parts[second] * factor
            if first == second:
                entry = entry + isotropic
            entries.append(entry)
        rows_list.append(jnp.stack(entries, axis=-1))
    return jnp.stack(rows_list, axis=1)


def draw_matrix(key, part):
    key = jax.random.fold_in(key, 11)
    key_x, key_y, key_z, key_shift, key_scale = jax.random.split(key, 5)
    count = (ORDER + 2) // 3
    side = (2.0 * count) ** (1.0 / 3.0)
    height = 0.5 * side
    px_pos = jax.random.uniform(key_x, (count,), jnp.float32, 0.0, side)
    py_pos = jax.random.uniform(key_y, (count,), jnp.float32, 0.0, side)
    lift = jax.random.uniform(key_z, (count,), jnp.float32, 0.0, 1.0)
    pz_pos = height * lift
    radius = 1.0
    shift = jax.random.uniform(key_shift, (ORDER,), jnp.float32, 0.3, 1.0)
    scales = jnp.exp(jax.random.uniform(key_scale, (ORDER,), jnp.float32, -0.69, 0.69))
    blocks = stokeslet_blocks(px_pos, py_pos, pz_pos, radius)
    whole = blocks.reshape(3 * count, 3 * count)[:ORDER, :ORDER]
    index = jnp.arange(ORDER)
    whole = whole.at[index, index].add(shift)
    whole = whole * (scales[:, None] * scales[None, :])
    return to_stored_draw(whole)


def setup_inputs(seed: int = 0) -> dict:
    seeds = jax.random.split(jax.random.key(seed), 2)
    matrix = draw_matrix(jax.random.fold_in(seeds[1], 71), 0)
    return {"matrix": matrix}


def to_global(stored):
    rows_tiles = TILES // N_ROW
    cols_tiles = TILES // N_COL
    shaped = stored.reshape(N_ROW, rows_tiles, TILE, N_COL, cols_tiles, TILE)
    return shaped.transpose(1, 0, 2, 4, 3, 5).reshape(ORDER, ORDER)

def to_stored(whole):
    rows_tiles = TILES // N_ROW
    cols_tiles = TILES // N_COL
    shaped = whole.reshape(rows_tiles, N_ROW, TILE, cols_tiles, N_COL, TILE)
    return shaped.transpose(1, 0, 2, 4, 3, 5).reshape(ORDER, ORDER)

def product_t(left, right):
    return lax.dot_general(left.astype(jnp.float32), right.astype(jnp.float32), (((1,), (1,)), ((), ())), precision=lax.Precision.HIGHEST, preferred_element_type=jnp.float32)

def one_panel(square):
    lower = jnp.linalg.cholesky(square[:TILE, :TILE])
    identity = jnp.eye(TILE, dtype=lower.dtype)
    inverse = lax.linalg.triangular_solve(lower, identity, left_side=True, lower=True)
    solved = product_t(square[TILE:, :TILE], inverse)
    trailing = square[TILE:, TILE:] - product_t(solved, solved)
    return (jnp.concatenate([lower, solved], axis=0), trailing)

def reference(matrix):
    whole = to_global(matrix)
    first_col, schur_one = one_panel(whole)
    second_col, schur_two = one_panel(schur_one)
    result = jnp.zeros((ORDER, ORDER), jnp.float32)
    result = result.at[:, :TILE].set(first_col)
    result = result.at[TILE:, TILE:2 * TILE].set(second_col)
    result = result.at[2 * TILE:, 2 * TILE:].set(schur_two)
    return to_stored(result)
```

```python
import functools

import jax
import jax.numpy as jnp
from jax import lax
from jax.experimental import pallas as pl
from jax.experimental.pallas import tpu as pltpu
from jax.sharding import PartitionSpec as P

TILE = 128
SUP = 64
SIDE = 1280
RING_X = 4
RING_Y = 4
RING_Z = 8
ZCH = 20
ZROWS = SIDE // ZCH
PCH = 5
LAG = 2
EXACT = lax.Precision.HIGHEST
MESH = pl.DeviceIdType.MESH


def dot(left, right, dims):
    return lax.dot_general(
        left, right, (dims, ((), ())), precision=EXACT, preferred_element_type=jnp.float32
    )


def cholesky_inverse(tile):
    sub = lax.broadcasted_iota(jnp.int32, (8, TILE), 0)
    lane = lax.broadcasted_iota(jnp.int32, (8, TILE), 1)
    count = TILE // 8
    a = [tile[8 * i : 8 * i + 8] for i in range(count)]
    w = [jnp.where(lane == sub + 8 * i, 1.0, 0.0) for i in range(count)]
    for start in range(0, TILE, SUP):
        blocks = list(range(start // 8, (start + SUP) // 8))
        for t in blocks:
            j0 = 8 * t
            rest = [m for m in blocks if m >= t]
            col = {
                m: [jnp.broadcast_to(a[m][:, j0 + q : j0 + q + 1], (8, TILE)) for q in range(8)]
                for m in rest
            }
            scale = jnp.zeros((8, TILE), jnp.float32)
            for p in range(8):
                root = lax.rsqrt(jnp.broadcast_to(col[t][p][p : p + 1], (8, TILE)))
                scale = jnp.where(sub == p, root, scale)
                row_a = jnp.broadcast_to(a[t][p : p + 1], (8, TILE)) * root
                row_w = jnp.broadcast_to(w[t][p : p + 1], (8, TILE)) * root
                piece = {
                    q: jnp.broadcast_to(col[t][q][p : p + 1], (8, TILE)) * root
                    for q in range(p + 1, 8)
                }
                for m in rest:
                    factor = col[m][p] * root
                    for q in range(p + 1, 8):
                        col[m][q] = col[m][q] - factor * piece[q]
                    if m == t:
                        factor = jnp.where(sub > p, factor, 0.0)
                    a[m] = a[m] - factor * row_a
                    w[m] = w[m] - factor * row_w
            a[t] = jnp.where(lane >= sub + j0, a[t] * scale, 0.0)
            w[t] = w[t] * scale
        end = start + SUP
        if end < TILE:
            upper = jnp.concatenate([a[m] for m in blocks], 0)
            both = jnp.concatenate([upper, jnp.concatenate([w[m] for m in blocks], 0)], 1)
            change = dot(upper, both, ((0,), (0,)))
            for m in range(end // 8, count):
                a[m] = a[m] - change[8 * m : 8 * m + 8, :TILE]
                w[m] = w[m] - change[8 * m : 8 * m + 8, TILE:]
    return jnp.concatenate(a, 0), jnp.concatenate(w, 0)


def place():
    r = lax.axis_index("row")
    c = lax.axis_index("col")
    return r % RING_X, r // RING_X, c // 2, c % 2


def device(x, y, z, k):
    return (y * RING_X + x, z * 2 + k)


def wrap(i, n):
    return lax.rem(i + n, n)


def panels_kernel(
    a_ref, pr_ref, pc_hi_ref, pc_lo_ref, u_ref,
    hr, hc, cn, w_all,
    cn_recv, cn_send, cn_sib, z_recv, z_send, z_sib_recv, z_sib_send, z_own,
    p_recv, px_send, py_send, p_own,
):
    x, y, z, k = place()
    r = y * RING_X + x
    flat = r
    sibling = device(x, y, z, 1 - k)
    pos = jnp.where(k == 0, z, wrap(RING_Z - z, RING_Z))
    step = 1 - 2 * k
    z_next = device(x, y, wrap(z + step, RING_Z), k)

    barrier = pltpu.get_barrier_semaphore()

    def greet(target):
        pl.semaphore_signal(barrier, inc=1, device_id=target, device_id_type=MESH)

    greet(sibling)
    greet(device(x, y, wrap(z + 1, RING_Z), k))
    greet(device(x, y, wrap(z - 1, RING_Z), k))
    greet(device(wrap(x + 1, RING_X), y, z, k))
    greet(device(wrap(x - 1, RING_X), y, z, k))
    greet(device(x, wrap(y + 1, RING_Y), z, k))
    greet(device(x, wrap(y - 1, RING_Y), z, k))
    root_here = [
        jnp.logical_and(flat == 0, k == 0),
        jnp.logical_and(flat == 0, k == 1),
        jnp.logical_and(flat == 1, k == 1),
    ]
    root_row = (0, 0, 1)
    root_core = (0, 1, 1)
    count = jnp.int32(7)
    for tile in range(3):
        mine = k == root_core[tile]

        @pl.when(jnp.logical_and(mine, flat != root_row[tile]))
        def _(tile=tile):
            greet((root_row[tile], z * 2 + root_core[tile]))

        @pl.when(jnp.logical_and(root_here[tile], z != 0))
        def _(tile=tile):
            greet((root_row[tile], root_core[tile]))

        count = count + jnp.where(root_here[tile], 15 + jnp.where(z == 0, 7, 0), 0)
    pl.semaphore_wait(barrier, count)

    def remote(src, dst, send, recv, target):
        return pltpu.make_async_remote_copy(
            src_ref=src, dst_ref=dst, send_sem=send, recv_sem=recv, device_id=target,
            device_id_type=MESH,
        )

    corner_src = a_ref.at[0:TILE, 0:TILE]
    for tile in range(3):

        @pl.when(jnp.logical_and(root_here[tile], z == 0))
        def _(tile=tile):
            @pl.loop(1, RING_Z)
            def _(i):
                remote(
                    corner_src, cn.at[tile], cn_send.at[tile], cn_recv.at[tile],
                    (root_row[tile], i * 2 + root_core[tile]),
                ).start()

            own = pltpu.make_async_copy(corner_src, cn.at[tile], cn_recv.at[tile])
            own.start()

    for tile in range(3):

        @pl.when(k == root_core[tile])
        def _(tile=tile):
            pltpu.make_async_copy(corner_src, cn.at[tile], cn_recv.at[tile]).wait()

            @pl.when(root_here[tile])
            def _():
                @pl.loop(1, 16)
                def _(i):
                    remote(
                        cn.at[tile], cn.at[tile], cn_send.at[tile], cn_recv.at[tile],
                        (wrap(root_row[tile] + i, 16), z * 2 + root_core[tile]),
                    ).start()

            remote(cn.at[tile], cn.at[tile], cn_sib.at[tile], cn_recv.at[tile], sibling).start()

    def z_chunk(j):
        rows = pl.ds(pl.multiple_of(j * ZROWS, ZROWS), ZROWS)
        here = hr.at[k, rows]

        def send(src):
            @pl.when(pos < RING_Z - 1)
            def _():
                remote(src, here, z_send, z_recv.at[j], z_next).start()

            remote(src, here, z_sib_send, z_sib_recv, sibling).start()

        @pl.when(pos == 0)
        def _():
            send(a_ref.at[rows, 0:TILE])

        @pl.when(pos != 0)
        def _():
            pltpu.make_async_copy(here, here, z_recv.at[j]).wait()
            send(here)

    def p_chunk(s, d, j):
        sign = 1 - 2 * d
        lanes = slice((d * PCH + j) * TILE, (d * PCH + j + 1) * TILE)
        here = hc.at[s, :, lanes]
        index = (s * 2 + d) * PCH + j
        xpos = wrap((x - s) * sign + RING_X, RING_X)
        ypos = wrap(y * sign, RING_Y)
        source = flat == s
        go_x = jnp.logical_and(xpos < RING_X - 1, jnp.logical_or(k == 1, y == 0))
        go_y = jnp.logical_and(ypos < RING_Y - 1, jnp.logical_or(k == 0, x == s))

        def send(src):
            @pl.when(go_x)
            def _():
                remote(
                    src, here, px_send.at[index], p_recv.at[index],
                    device(wrap(x + sign, RING_X), y, z, k),
                ).start()

            @pl.when(go_y)
            def _():
                remote(
                    src, here, py_send.at[index], p_recv.at[index],
                    device(x, wrap(y + sign, RING_Y), z, k),
                ).start()

        @pl.when(source)
        def _():
            send(a_ref.at[0:TILE, lanes])

        @pl.when(jnp.logical_not(source))
        def _():
            pltpu.make_async_copy(here, here, p_recv.at[index]).wait()
            send(here)

    @pl.when(pos == 0)
    def _():
        pltpu.make_async_copy(a_ref.at[:, 0:TILE], hr.at[k], z_own).start()

    @pl.when(flat < 2)
    def _():
        pltpu.make_async_copy(a_ref.at[0:TILE, :], hc.at[flat], p_own).start()

    hops = {}
    for s in range(2):
        for d in range(2):
            sign = 1 - 2 * d
            hops[s, d] = wrap((x - s) * sign + RING_X, RING_X) + wrap(y * sign, RING_Y)

    slots = ZCH + LAG * (RING_Z - 1)
    for slot in range(slots):
        j = slot - LAG * pos

        @pl.when(jnp.logical_and(j >= 0, j < ZCH))
        def _(j=j):
            z_chunk(j)

        for s in range(2):
            for d in range(2):
                for jj in range(PCH):
                    at = slot - 4 * jj - 2 * s - d
                    if 0 <= at <= LAG * 6 and at % LAG == 0:

                        @pl.when(hops[s, d] == at // LAG)
                        def _(s=s, d=d, jj=jj):
                            p_chunk(s, d, jj)

    for tile in range(3):

        @pl.when(k != root_core[tile])
        def _(tile=tile):
            pltpu.make_async_copy(cn.at[tile], cn.at[tile], cn_recv.at[tile]).wait()

        @pl.when(k == root_core[tile])
        def _(tile=tile):
            remote(cn.at[tile], cn.at[tile], cn_sib.at[tile], cn_recv.at[tile], sibling).wait_send()

            def drain(n):
                @pl.loop(0, n)
                def _(i):
                    remote(
                        cn.at[tile], cn.at[tile], cn_send.at[tile], cn_recv.at[tile], sibling
                    ).wait_send()

            @pl.when(root_here[tile])
            def _():
                drain(15)

            @pl.when(jnp.logical_and(root_here[tile], z == 0))
            def _():
                drain(7)

    u0, w0 = cholesky_inverse(cn[0])
    u01 = dot(w0, cn[1], ((1,), (0,)))
    u1, w1 = cholesky_inverse(cn[2] - dot(u01, u01, ((0,), (0,))))
    w10 = -dot(w1, dot(u01, w0, ((0,), (0,))), ((1,), (0,)))
    w_all[:TILE, :TILE] = w0
    w_all[:TILE, TILE:] = jnp.zeros((TILE, TILE), jnp.float32)
    w_all[TILE:, :TILE] = w10
    w_all[TILE:, TILE:] = w1
    u_ref[0] = u0.T
    u_ref[1] = u1.T

    whole_r = hr.at[k]
    other_r = hr.at[1 - k]
    pltpu.make_async_copy(other_r, other_r, z_sib_recv).wait()

    @pl.when(pos == 0)
    def _():
        pltpu.make_async_copy(a_ref.at[:, 0:TILE], hr.at[k], z_own).wait()

    @pl.when(flat < 2)
    def _():
        pltpu.make_async_copy(a_ref.at[0:TILE, :], hc.at[flat], p_own).wait()

    @pl.loop(0, SIDE // 256)
    def _(i):
        rows = pl.ds(pl.multiple_of(i * 256, 256), 256)
        raw = jnp.concatenate([hr[0, rows], hr[1, rows]], axis=1)
        pr_ref[rows] = dot(raw, w_all[...], ((1,), (1,)))

    for i in range(SIDE // 256):
        lanes = slice(i * 256, i * 256 + 256)
        raw = jnp.concatenate([hc[0, :, lanes], hc[1, :, lanes]], axis=0)
        got = dot(w_all[...], raw, ((1,), (0,)))
        high = got.astype(jnp.bfloat16)
        pc_hi_ref[:, lanes] = high
        pc_lo_ref[:, lanes] = (got - high.astype(jnp.float32)).astype(jnp.bfloat16)

    remote(whole_r, whole_r, z_sib_send, z_sib_recv, sibling).wait_send()

    @pl.when(pos < RING_Z - 1)
    def _():
        remote(whole_r, whole_r, z_send, z_sib_recv, sibling).wait_send()

    for s in range(2):
        for d in range(2):
            sign = 1 - 2 * d
            xpos = wrap((x - s) * sign + RING_X, RING_X)
            ypos = wrap(y * sign, RING_Y)
            go_x = jnp.logical_and(xpos < RING_X - 1, jnp.logical_or(k == 1, y == 0))
            go_y = jnp.logical_and(ypos < RING_Y - 1, jnp.logical_or(k == 0, x == s))
            for jj in range(PCH):
                index = (s * 2 + d) * PCH + jj
                here = hc.at[s, :, (d * PCH + jj) * TILE : (d * PCH + jj + 1) * TILE]

                @pl.when(go_x)
                def _(here=here, index=index):
                    remote(here, here, px_send.at[index], p_recv.at[index], sibling).wait_send()

                @pl.when(go_y)
                def _(here=here, index=index):
                    remote(here, here, py_send.at[index], p_recv.at[index], sibling).wait_send()


def panels(matrix):
    vmem = pl.BlockSpec(memory_space=pltpu.VMEM)
    f32 = jnp.float32
    dma = pltpu.SemaphoreType.DMA
    return pl.pallas_call(
        panels_kernel,
        out_shape=[
            jax.ShapeDtypeStruct((SIDE, 2 * TILE), f32),
            jax.ShapeDtypeStruct((2 * TILE, SIDE), jnp.bfloat16),
            jax.ShapeDtypeStruct((2 * TILE, SIDE), jnp.bfloat16),
            jax.ShapeDtypeStruct((2, TILE, TILE), f32),
        ],
        in_specs=[pl.BlockSpec(memory_space=pl.ANY)],
        out_specs=[vmem] * 4,
        scratch_shapes=[
            pltpu.VMEM((2, SIDE, TILE), f32),
            pltpu.VMEM((2, TILE, SIDE), f32),
            pltpu.VMEM((3, TILE, TILE), f32),
            pltpu.VMEM((2 * TILE, 2 * TILE), f32),
            dma((3,)), dma((3,)), dma((3,)),
            dma((ZCH,)), dma, dma, dma, dma,
            dma((4 * PCH,)), dma((4 * PCH,)), dma((4 * PCH,)), dma,
        ],
        compiler_params=pltpu.CompilerParams(
            collective_id=0, has_side_effects=True, vmem_limit_bytes=40 * 2**20
        ),
        name="panels",
    )(matrix)


def update_kernel(a_ref, pr_ref, pc_hi_ref, pc_lo_ref, u_ref, out_ref):
    i = pl.program_id(0)
    r = lax.axis_index("row")
    c = lax.axis_index("col")
    high = pr_ref[...].astype(jnp.bfloat16)
    low = (pr_ref[...] - high.astype(jnp.float32)).astype(jnp.bfloat16)

    def part(left, right):
        return lax.dot_general(
            left, right[...], (((1,), (0,)), ((), ())), preferred_element_type=jnp.float32
        )

    out_ref[...] = a_ref[...] - (
        part(high, pc_hi_ref) + (part(high, pc_lo_ref) + part(low, pc_hi_ref))
    )

    @pl.when(c == 0)
    def _():
        out_ref[:, :TILE] = pr_ref[:, :TILE]

    @pl.when(c == 1)
    def _():
        out_ref[:, :TILE] = pr_ref[:, TILE:]

    @pl.when(jnp.logical_and(i == 0, r < 2))
    def _():
        @pl.when(jnp.logical_or(c != 0, r == 0))
        def _():
            out_ref[:TILE, :TILE] = jnp.where(c == r, u_ref[r], 0.0)

        out_ref[:TILE, TILE:] = jnp.zeros((TILE, SIDE - TILE), jnp.float32)


def update(matrix, pr, pc_hi, pc_lo, u):
    rows = 256
    return pl.pallas_call(
        update_kernel,
        grid=(SIDE // rows,),
        out_shape=jax.ShapeDtypeStruct((SIDE, SIDE), jnp.float32),
        in_specs=[
            pl.BlockSpec((rows, SIDE), lambda i: (i, 0)),
            pl.BlockSpec((rows, 2 * TILE), lambda i: (i, 0)),
            pl.BlockSpec((2 * TILE, SIDE), lambda i: (0, 0)),
            pl.BlockSpec((2 * TILE, SIDE), lambda i: (0, 0)),
            pl.BlockSpec((2, TILE, TILE), lambda i: (0, 0, 0)),
        ],
        out_specs=pl.BlockSpec((rows, SIDE), lambda i: (i, 0)),
        compiler_params=pltpu.CompilerParams(vmem_limit_bytes=40 * 2**20),
        name="update",
    )(matrix, pr, pc_hi, pc_lo, u)


def per_device(matrix):
    return update(matrix, *panels(matrix))


def solution(mesh):
    return jax.shard_map(
        per_device, mesh=mesh, in_specs=(P("row", "col"),), out_specs=P("row", "col"),
        check_vma=False,
    )
```

```python
import functools

import jax
import jax.numpy as jnp
from jax import lax
from jax.experimental import pallas as pl
from jax.experimental.pallas import tpu as pltpu
from jax.sharding import PartitionSpec as P

TILE = 128
SUP = 64
SIDE = 1280
RING_X = 4
RING_Y = 4
RING_Z = 8
ZCH = 8
ZROWS = SIDE // ZCH
PCH = 4
PROWS = TILE // 4 // PCH
FIRST = 18
UROWS = 128
VMEM_LIMIT = 40 * 2**20
UPDATE_LIMIT = 24 * 2**20
EXACT = lax.Precision.HIGHEST
MESH = pl.DeviceIdType.MESH


def dot(left, right, dims):
    return lax.dot_general(
        left, right, (dims, ((), ())), precision=EXACT, preferred_element_type=jnp.float32
    )


def cholesky_inverse(tile):
    sub = lax.broadcasted_iota(jnp.int32, (8, TILE), 0)
    lane = lax.broadcasted_iota(jnp.int32, (8, TILE), 1)
    count = TILE // 8
    a = [tile[8 * i : 8 * i + 8] for i in range(count)]
    w = [jnp.where(lane == sub + 8 * i, 1.0, 0.0) for i in range(count)]
    for start in range(0, TILE, SUP):
        blocks = list(range(start // 8, (start + SUP) // 8))
        for t in blocks:
            j0 = 8 * t
            rest = [m for m in blocks if m >= t]
            col = {
                m: [jnp.broadcast_to(a[m][:, j0 + q : j0 + q + 1], (8, TILE)) for q in range(8)]
                for m in rest
            }
            scale = jnp.zeros((8, TILE), jnp.float32)
            for p in range(8):
                root = lax.rsqrt(jnp.broadcast_to(col[t][p][p : p + 1], (8, TILE)))
                scale = jnp.where(sub == p, root, scale)
                row_a = jnp.broadcast_to(a[t][p : p + 1], (8, TILE)) * root
                row_w = jnp.broadcast_to(w[t][p : p + 1], (8, TILE)) * root
                piece = {
                    q: jnp.broadcast_to(col[t][q][p : p + 1], (8, TILE)) * root
                    for q in range(p + 1, 8)
                }
                for m in rest:
                    factor = col[m][p] * root
                    for q in range(p + 1, 8):
                        col[m][q] = col[m][q] - factor * piece[q]
                    if m == t:
                        factor = jnp.where(sub > p, factor, 0.0)
                    a[m] = a[m] - factor * row_a
                    w[m] = w[m] - factor * row_w
            a[t] = jnp.where(lane >= sub + j0, a[t] * scale, 0.0)
            w[t] = w[t] * scale
        end = start + SUP
        if end < TILE:
            upper = jnp.concatenate([a[m] for m in blocks], 0)
            both = jnp.concatenate([upper, jnp.concatenate([w[m] for m in blocks], 0)], 1)
            change = dot(upper, both, ((0,), (0,)))
            for m in range(end // 8, count):
                a[m] = a[m] - change[8 * m : 8 * m + 8, :TILE]
                w[m] = w[m] - change[8 * m : 8 * m + 8, TILE:]
    return jnp.concatenate(a, 0), jnp.concatenate(w, 0)


def place():
    r = lax.axis_index("row")
    c = lax.axis_index("col")
    return r % RING_X, r // RING_X, c // 2, c % 2


def device(x, y, z, k):
    return (y * RING_X + x, z * 2 + k)


def wrap(i, n):
    return lax.rem(i + n, n)


TREE = {
    (0, 0): (0,), (1, 0): (0, 1, 3), (2, 0): (0, 3), (1, 1): (0, 1, 2), (1, 3): (2,),
    (2, 1): (0, 1), (2, 3): (0,), (1, 2): (2,), (2, 2): (0,),
}
LEVEL = {(0, 0): 0, (1, 0): 1, (2, 0): 2, (1, 1): 2, (1, 3): 2, (2, 1): 3, (2, 3): 3, (1, 2): 3, (2, 2): 4}
STEPS = ((1, 0), (0, 1), (-1, 0), (0, -1))
HOP = 3


def panels_kernel(
    a_ref, a_out, pr_ref, pc_hi_ref, pc_lo_ref,
    hr, hc, cn, w_all,
    cn_recv, cn_send, cn_sib, z_recv, z_send, z_sib_recv, z_sib_send, z_own,
    p_recv, p_send, p_own, a_sem,
):
    x, y, z, k = place()
    r = y * RING_X + x
    sibling = device(x, y, z, 1 - k)
    step = 1 - 2 * k
    pos = jnp.where(k == 0, z, wrap(RING_Z - z, RING_Z))
    around = (
        device(wrap(x + 1, RING_X), y, z, k),
        device(x, wrap(y + 1, RING_Y), z, k),
        device(wrap(x - 1, RING_X), y, z, k),
        device(x, wrap(y - 1, RING_Y), z, k),
    )
    z_next = device(x, y, wrap(z + step, RING_Z), k)
    z_prev = device(x, y, wrap(z - step, RING_Z), k)
    z_skip = device(x, y, wrap(z + 2 * step, RING_Z), k)
    z_back = device(x, y, wrap(z - 2 * step, RING_Z), k)
    x_far = device(wrap(x + 2, RING_X), y, z, k)
    y_far = device(x, wrap(y + 2, RING_Y), z, k)

    pltpu.make_async_copy(a_ref, a_out, a_sem).start()
    barrier = pltpu.get_barrier_semaphore()

    def greet(target):
        pl.semaphore_signal(barrier, inc=1, device_id=target, device_id_type=MESH)

    for target in (sibling, z_next, z_prev, x_far, y_far) + around:
        greet(target)

    @pl.when(pos == 4)
    def _():
        greet(z_back)

    root_core = (0, 1, 1)
    root_x = (0, 0, 1)
    count = 9 + jnp.where(pos == 2, 1, 0)
    for tile in range(3):
        in_ring = jnp.logical_and(jnp.logical_and(x == root_x[tile], y == 0), k == root_core[tile])

        @pl.when(jnp.logical_and(in_ring, z != 0))
        def _(tile=tile):
            greet((root_x[tile], root_core[tile]))

        count = count + jnp.where(jnp.logical_and(in_ring, z == 0), 7, 0)
    pl.semaphore_wait(barrier, count)

    def remote(src, dst, send, recv, target):
        return pltpu.make_async_remote_copy(
            src_ref=src, dst_ref=dst, send_sem=send, recv_sem=recv, device_id=target,
            device_id_type=MESH,
        )

    corner_src = a_ref.at[0:TILE, 0:TILE]

    def corner_z(tile):
        mine = jnp.logical_and(jnp.logical_and(x == root_x[tile], y == 0), k == root_core[tile])

        @pl.when(jnp.logical_and(mine, z == 0))
        def _():
            for i in range(1, RING_Z):
                remote(
                    corner_src, cn.at[tile], cn_send.at[tile, i - 1], cn_recv.at[tile],
                    (root_x[tile], i * 2 + root_core[tile]),
                ).start()
            pltpu.make_async_copy(corner_src, cn.at[tile], cn_recv.at[tile]).start()

    def corner_wait(tile):
        pltpu.make_async_copy(corner_src, cn.at[tile], cn_recv.at[tile]).wait()

    def corner_send(tile, sem, target):
        remote(cn.at[tile], cn.at[tile], cn_send.at[tile, sem], cn_recv.at[tile], target).start()

    def corner_x(tile):
        mine = jnp.logical_and(jnp.logical_and(x == root_x[tile], y == 0), k == root_core[tile])

        @pl.when(mine)
        def _():
            corner_wait(tile)
            corner_send(tile, 7, around[0])
            corner_send(tile, 8, around[2])
            corner_send(tile, 9, x_far)
            corner_send(tile, 10, around[1])
            corner_send(tile, 11, around[3])
            corner_send(tile, 12, y_far)
            remote(cn.at[tile], cn.at[tile], cn_sib.at[tile], cn_recv.at[tile], sibling).start()

    def corner_y(tile):
        mine = jnp.logical_and(k == root_core[tile], jnp.logical_and(y == 0, x != root_x[tile]))

        @pl.when(mine)
        def _():
            corner_wait(tile)
            corner_send(tile, 10, around[1])
            corner_send(tile, 11, around[3])
            corner_send(tile, 12, y_far)
            remote(cn.at[tile], cn.at[tile], cn_sib.at[tile], cn_recv.at[tile], sibling).start()

    def corner_end(tile):
        @pl.when(jnp.logical_and(k == root_core[tile], y != 0))
        def _():
            corner_wait(tile)
            remote(cn.at[tile], cn.at[tile], cn_sib.at[tile], cn_recv.at[tile], sibling).start()

        @pl.when(k != root_core[tile])
        def _():
            corner_wait(tile)

    def corner_drain(tile):
        mine = k == root_core[tile]
        here = cn.at[tile]

        def sent(sem):
            remote(here, here, sem, cn_recv.at[tile], sibling).wait_send()

        @pl.when(mine)
        def _():
            sent(cn_sib.at[tile])

            @pl.when(y == 0)
            def _():
                for i in (10, 11, 12):
                    sent(cn_send.at[tile, i])

            @pl.when(jnp.logical_and(y == 0, x == root_x[tile]))
            def _():
                for i in (7, 8, 9):
                    sent(cn_send.at[tile, i])

                @pl.when(z == 0)
                def _():
                    for i in range(7):
                        sent(cn_send.at[tile, i])

    def z_rows(j):
        return pl.ds(j * ZROWS, ZROWS)

    def z_send_chunk(j, way, src, target):
        remote(src, hr.at[k, z_rows(j)], z_send.at[way], z_recv.at[j], target).start()

    def z_sibling(j, src):
        remote(src, hr.at[k, z_rows(j)], z_sib_send, z_sib_recv, sibling).start()

    def z_service(j, place_here):
        @pl.when(pos == place_here)
        def _():
            here = hr.at[k, z_rows(j)]
            pltpu.make_async_copy(here, here, z_recv.at[j]).wait()
            if place_here in (1, 2, 4):
                z_send_chunk(j, 0, here, z_next)
            if place_here == 2:
                z_send_chunk(j, 1, here, z_skip)
            if place_here == 7:
                z_send_chunk(j, 0, here, z_prev)
            z_sibling(j, here)

    whole_r = hr.at[k]

    def z_sent(way):
        remote(whole_r, whole_r, z_send.at[way], z_sib_recv, sibling).wait_send()

    trees = []
    for s in range(2):
        for d in range(4):
            fx, fy = wrap(x - s + RING_X, RING_X), y
            for _ in range(d):
                fx, fy = fy, wrap(RING_X - fx, RING_X)
            at = fx + RING_X * fy
            trees.append((s, d, at))

    def p_rows(d, j):
        start = d * (TILE // 4) + j * PROWS
        return slice(start, start + PROWS)

    def p_service(index, j, level):
        s, d, at = trees[index]
        here = hc.at[s, p_rows(d, j)]
        for spot, ways in TREE.items():
            if LEVEL[spot] != level:
                continue

            @pl.when(at == spot[0] + RING_X * spot[1])
            def _(ways=ways):
                if level == 0:
                    src = a_ref.at[p_rows(d, j)]
                else:
                    src = here
                    pltpu.make_async_copy(here, here, p_recv.at[index, j]).wait()
                for way in ways:
                    remote(
                        src, here, p_send.at[index, way], p_recv.at[index, j],
                        around[(way + d) % 4],
                    ).start()

    def p_end(index):
        s, d, at = trees[index]
        inner = [spot[0] + RING_X * spot[1] for spot in TREE]
        leaf = at != inner[0]
        for spot in inner[1:]:
            leaf = jnp.logical_and(leaf, at != spot)
        for j in range(PCH):
            here = hc.at[s, p_rows(d, j)]

            @pl.when(leaf)
            def _(here=here, j=j):
                pltpu.make_async_copy(here, here, p_recv.at[index, j]).wait()

    def p_drain(index):
        s, d, at = trees[index]
        part = hc.at[s, d * (TILE // 4) : (d + 1) * (TILE // 4)]
        for spot, ways in TREE.items():

            @pl.when(at == spot[0] + RING_X * spot[1])
            def _(ways=ways):
                for way in ways:
                    remote(
                        part, part, p_send.at[index, way], p_recv.at[index, 0], sibling
                    ).wait_send()

    for tile in range(3):
        corner_z(tile)

    @pl.when(pos == 0)
    def _():
        for j in range(ZCH):
            z_send_chunk(j, 0, a_ref.at[z_rows(j), 0:TILE], z_next)
        for j in range(ZCH):
            z_sibling(j, a_ref.at[z_rows(j), 0:TILE])
        pltpu.make_async_copy(a_ref.at[:, 0:TILE], hr.at[k], z_own).start()

    for j in range(PCH):
        for index in range(8):
            p_service(index, j, 0)

    @pl.when(r < 2)
    def _():
        pltpu.make_async_copy(a_ref.at[0:TILE, :], hc.at[r], p_own).start()

    def second_wave():
        @pl.when(pos == 0)
        def _():
            z_sent(0)
            for j in range(ZCH):
                z_send_chunk(j, 1, a_ref.at[z_rows(j), 0:TILE], z_prev)

    z_level = {1: 0, 2: 1, 3: 2, 4: 2, 5: 3, 7: 3, 6: 4}
    def slot_work(slot):
        if slot == 4:
            for tile in range(3):
                corner_x(tile)
        if slot == 7:
            second_wave()
        if slot == 8:
            for tile in range(3):
                corner_y(tile)
        for j in range(PCH):
            for level in range(1, 5):
                if HOP * level + 2 * j == slot:
                    for index in range(8):
                        p_service(index, j, level)
        for j in range(ZCH):
            for where_, level in ((1, 1), (2, 2), (3, 3), (4, 3), (5, 4)):
                if HOP * level + j == slot:
                    z_service(j, where_)
            for where_, level in ((7, 1), (6, 2)):
                if 8 + HOP * level + j == slot:
                    z_service(j, where_)

    for slot in range(1, FIRST):
        slot_work(slot)

    corner_end(0)
    u0, w0 = cholesky_inverse(cn[0])
    w_all[:TILE, :TILE] = w0
    w_all[:TILE, TILE:] = jnp.zeros((TILE, TILE), jnp.float32)
    corner_end(1)
    corner_end(2)
    u01 = dot(w_all[:TILE, :TILE], cn[1], ((1,), (0,)))
    for slot in range(FIRST, 25):
        slot_work(slot)
    u1, w1 = cholesky_inverse(cn[2] - dot(u01, u01, ((0,), (0,))))
    w10 = -dot(w1, dot(u01, w_all[:TILE, :TILE], ((0,), (0,))), ((1,), (0,)))
    w_all[TILE:, :TILE] = w10
    w_all[TILE:, TILE:] = w1

    other_r = hr.at[1 - k]
    pltpu.make_async_copy(other_r, other_r, z_sib_recv).wait()

    @pl.when(pos == 0)
    def _():
        pltpu.make_async_copy(a_ref.at[:, 0:TILE], hr.at[k], z_own).wait()

    @pl.when(r < 2)
    def _():
        pltpu.make_async_copy(a_ref.at[0:TILE, :], hc.at[r], p_own).wait()

    for index in range(8):
        p_end(index)

    @pl.loop(0, SIDE // 256)
    def _(i):
        rows = pl.ds(pl.multiple_of(i * 256, 256), 256)
        raw = jnp.concatenate([hr[0, rows], hr[1, rows]], axis=1)
        pr_ref[rows] = dot(raw, w_all[...], ((1,), (1,)))

    for i in range(SIDE // 256):
        lanes = slice(i * 256, i * 256 + 256)
        raw = jnp.concatenate([hc[0, :, lanes], hc[1, :, lanes]], axis=0)
        got = dot(w_all[...], raw, ((1,), (0,)))
        high = got.astype(jnp.bfloat16)
        pc_hi_ref[:, lanes] = high
        pc_lo_ref[:, lanes] = (got - high.astype(jnp.float32)).astype(jnp.bfloat16)

    for tile in range(3):
        corner_drain(tile)
    remote(whole_r, whole_r, z_sib_send, z_sib_recv, sibling).wait_send()

    @pl.when(jnp.logical_or(jnp.logical_or(pos == 1, pos == 2), jnp.logical_or(pos == 4, pos == 7)))
    def _():
        z_sent(0)

    @pl.when(jnp.logical_or(pos == 0, pos == 2))
    def _():
        z_sent(1)

    for index in range(8):
        p_drain(index)
    pltpu.make_async_copy(a_ref, a_out, a_sem).wait()


def panels(matrix):
    vmem = pl.BlockSpec(memory_space=pltpu.VMEM)
    f32 = jnp.float32
    dma = pltpu.SemaphoreType.DMA
    return pl.pallas_call(
        panels_kernel,
        out_shape=[
            pltpu.VMEM((SIDE, SIDE), f32),
            pltpu.VMEM((SIDE, 2 * TILE), f32),
            pltpu.VMEM((2 * TILE, SIDE), jnp.bfloat16),
            pltpu.VMEM((2 * TILE, SIDE), jnp.bfloat16),
        ],
        in_specs=[pl.BlockSpec(memory_space=pl.ANY)],
        out_specs=[vmem] * 4,
        scratch_shapes=[
            pltpu.VMEM((2, SIDE, TILE), f32),
            pltpu.VMEM((2, TILE, SIDE), f32),
            pltpu.VMEM((3, TILE, TILE), f32),
            pltpu.VMEM((2 * TILE, 2 * TILE), f32),
            dma((3,)), dma((3, 13)), dma((3,)),
            dma((ZCH,)), dma((2,)), dma, dma, dma,
            dma((8, PCH)), dma((8, 4)), dma, dma,
        ],
        compiler_params=pltpu.CompilerParams(
            collective_id=0, has_side_effects=True, vmem_limit_bytes=VMEM_LIMIT
        ),
        name="panels",
    )(matrix)


def update_kernel(a_ref, pr_ref, pc_hi_ref, pc_lo_ref, out_ref, stage, sem):
    r = lax.axis_index("row")
    c = lax.axis_index("col")

    def part(left, right):
        return lax.dot_general(
            left, right[...], (((1,), (0,)), ((), ())), preferred_element_type=jnp.float32
        )

    for i in range(SIDE // UROWS):
        rows = slice(i * UROWS, (i + 1) * UROWS)
        high = pr_ref[rows].astype(jnp.bfloat16)
        low = (pr_ref[rows] - high.astype(jnp.float32)).astype(jnp.bfloat16)
        stage[rows] = a_ref[rows] - (
            part(high, pc_hi_ref) + (part(high, pc_lo_ref) + part(low, pc_hi_ref))
        )

        @pl.when(c == 0)
        def _(rows=rows):
            stage[rows, :TILE] = pr_ref[rows, :TILE]

        @pl.when(c == 1)
        def _(rows=rows):
            stage[rows, :TILE] = pr_ref[rows, TILE:]

        if i == 0:

            @pl.when(r < 2)
            def _():
                row = lax.broadcasted_iota(jnp.int32, (TILE, TILE), 0)
                lane = lax.broadcasted_iota(jnp.int32, (TILE, TILE), 1)
                kept = jnp.logical_or(c < r, jnp.logical_and(c == r, lane <= row))
                stage[:TILE, :TILE] = jnp.where(kept, stage[:TILE, :TILE], 0.0)
                stage[:TILE, TILE:] = jnp.zeros((TILE, SIDE - TILE), jnp.float32)

        pltpu.make_async_copy(stage.at[rows], out_ref.at[rows], sem.at[i]).start()
    for i in range(SIDE // UROWS):
        rows = slice(i * UROWS, (i + 1) * UROWS)
        pltpu.make_async_copy(stage.at[rows], out_ref.at[rows], sem.at[i]).wait()


def update(a, pr, pc_hi, pc_lo):
    vmem = pl.BlockSpec(memory_space=pltpu.VMEM)
    return pl.pallas_call(
        update_kernel,
        out_shape=jax.ShapeDtypeStruct((SIDE, SIDE), jnp.float32),
        in_specs=[vmem] * 4,
        out_specs=pl.BlockSpec(memory_space=pl.ANY),
        scratch_shapes=[
            pltpu.VMEM((SIDE, SIDE), jnp.float32), pltpu.SemaphoreType.DMA((SIDE // UROWS,)),
        ],
        compiler_params=pltpu.CompilerParams(vmem_limit_bytes=UPDATE_LIMIT),
        name="update",
    )(a, pr, pc_hi, pc_lo)


def per_device(matrix):
    return update(*panels(matrix))


def solution(mesh):
    return jax.shard_map(
        per_device, mesh=mesh, in_specs=(P("row", "col"),), out_specs=P("row", "col"),
        check_vma=False,
    )
```

```python
import functools

import jax
import jax.numpy as jnp
from jax import lax
from jax.experimental import pallas as pl
from jax.experimental.pallas import tpu as pltpu
from jax.sharding import PartitionSpec as P

TILE = 128
SUP = 64
SIDE = 1280
RING_X = 4
RING_Y = 4
RING_Z = 8
ZCH = 16
ZROWS = SIDE // ZCH
PCH = 4
PROWS = TILE // 4 // PCH
FIRST = 11
CX = {4: (0,), 7: (1, 2)}
CY = {8: (0,), 11: (1, 2)}
PC_SLOT = 20
PER_SLOT = 3
VMEM_LIMIT = 40 * 2**20
UPDATE_LIMIT = 24 * 2**20
EXACT = lax.Precision.HIGHEST
MESH = pl.DeviceIdType.MESH


def dot(left, right, dims):
    return lax.dot_general(
        left, right, (dims, ((), ())), precision=EXACT, preferred_element_type=jnp.float32
    )


def panel_dot(left, right, dims):
    def split(value):
        high = value.astype(jnp.bfloat16)
        return high, (value - high.astype(jnp.float32)).astype(jnp.bfloat16)

    def part(a, b):
        return lax.dot_general(a, b, (dims, ((), ())), preferred_element_type=jnp.float32)

    left_high, left_low = split(left)
    right_high, right_low = split(right)
    return part(left_high, right_high) + (part(left_high, right_low) + part(left_low, right_high))


def cholesky_inverse(tile):
    sub = lax.broadcasted_iota(jnp.int32, (8, TILE), 0)
    lane = lax.broadcasted_iota(jnp.int32, (8, TILE), 1)
    count = TILE // 8
    a = [tile[8 * i : 8 * i + 8] for i in range(count)]
    w = [jnp.where(lane == sub + 8 * i, 1.0, 0.0) for i in range(count)]
    for start in range(0, TILE, SUP):
        blocks = list(range(start // 8, (start + SUP) // 8))
        for t in blocks:
            j0 = 8 * t
            rest = [m for m in blocks if m >= t]
            col = {
                m: [jnp.broadcast_to(a[m][:, j0 + q : j0 + q + 1], (8, TILE)) for q in range(8)]
                for m in rest
            }
            scale = jnp.zeros((8, TILE), jnp.float32)
            for p in range(8):
                root = lax.rsqrt(jnp.broadcast_to(col[t][p][p : p + 1], (8, TILE)))
                scale = jnp.where(sub == p, root, scale)
                row_a = jnp.broadcast_to(a[t][p : p + 1], (8, TILE)) * root
                row_w = jnp.broadcast_to(w[t][p : p + 1], (8, TILE)) * root
                piece = {
                    q: jnp.broadcast_to(col[t][q][p : p + 1], (8, TILE)) * root
                    for q in range(p + 1, 8)
                }
                for m in rest:
                    factor = col[m][p] * root
                    for q in range(p + 1, 8):
                        col[m][q] = col[m][q] - factor * piece[q]
                    if m == t:
                        factor = jnp.where(sub > p, factor, 0.0)
                    a[m] = a[m] - factor * row_a
                    w[m] = w[m] - factor * row_w
            a[t] = a[t] * scale
            w[t] = w[t] * scale
            yield
        end = start + SUP
        if end < TILE:
            upper = jnp.concatenate([a[m] for m in blocks], 0)
            both = jnp.concatenate([upper, jnp.concatenate([w[m] for m in blocks], 0)], 1)
            change = dot(upper, both, ((0,), (0,)))
            for m in range(end // 8, count):
                a[m] = a[m] - change[8 * m : 8 * m + 8, :TILE]
                w[m] = w[m] - change[8 * m : 8 * m + 8, TILE:]
            yield
    return jnp.concatenate(w, 0)


def place():
    r = lax.axis_index("row")
    c = lax.axis_index("col")
    return r % RING_X, r // RING_X, c // 2, c % 2


def device(x, y, z, k):
    return (y * RING_X + x, z * 2 + k)


def wrap(i, n):
    return lax.rem(i + n, n)


TREE = {
    (0, 0): (0,), (1, 0): (0, 1, 3), (2, 0): (0, 3), (1, 1): (0, 1, 2), (1, 3): (2,),
    (2, 1): (0, 1, 4), (2, 3): (0,), (1, 2): (2,),
}
LEVEL = {(0, 0): 0, (1, 0): 1, (2, 0): 2, (1, 1): 2, (1, 3): 2, (2, 1): 3, (2, 3): 3, (1, 2): 3}
STEPS = ((1, 0), (0, 1), (-1, 0), (0, -1))
HOP = 3
Z_FAN = {0: (2, 6), 2: (1, 3, 4), 6: (5, 7)}


def panels_kernel(
    a_ref, a_out, pr_ref, pc_hi_ref, pc_lo_ref,
    hr, hc, cn, w_all,
    cn_recv, cn_send, cn_sib, z_recv, z_send, z_sib_recv, z_sib_send, z_own,
    p_recv, p_send, p_own, a_sem,
):
    x, y, z, k = place()
    r = y * RING_X + x
    sibling = device(x, y, z, 1 - k)
    step = 1 - 2 * k
    pos = jnp.where(k == 0, z, wrap(RING_Z - z, RING_Z))
    around = (
        device(wrap(x + 1, RING_X), y, z, k),
        device(x, wrap(y + 1, RING_Y), z, k),
        device(wrap(x - 1, RING_X), y, z, k),
        device(x, wrap(y - 1, RING_Y), z, k),
    )
    corners = tuple(
        device(wrap(x + dx, RING_X), wrap(y + dy, RING_Y), z, k)
        for dx, dy in ((1, 1), (-1, 1), (-1, -1), (1, -1))
    )
    z_next = device(x, y, wrap(z + step, RING_Z), k)
    z_prev = device(x, y, wrap(z - step, RING_Z), k)
    z_skip = device(x, y, wrap(z + 2 * step, RING_Z), k)
    z_back = device(x, y, wrap(z - 2 * step, RING_Z), k)
    x_far = device(wrap(x + 2, RING_X), y, z, k)
    y_far = device(x, wrap(y + 2, RING_Y), z, k)

    pltpu.make_async_copy(a_ref, a_out, a_sem).start()
    barrier = pltpu.get_barrier_semaphore()

    def greet(target):
        pl.semaphore_signal(barrier, inc=1, device_id=target, device_id_type=MESH)

    for target in (sibling, z_next, z_prev, x_far, y_far) + around + corners:
        greet(target)

    @pl.when(pos == 4)
    def _():
        greet(z_back)

    root_core = (0, 0, 1)
    root_x = (0, 1, 1)
    count = 13 + jnp.where(pos == 2, 1, 0)
    for tile in range(3):
        in_ring = jnp.logical_and(jnp.logical_and(x == root_x[tile], y == 0), k == root_core[tile])

        def greet_ring(where_, place_z, tile=tile, in_ring=in_ring):
            @pl.when(jnp.logical_and(in_ring, where_))
            def _():
                greet((root_x[tile], place_z * 2 + root_core[tile]))

        if tile == 0:
            greet_ring(z != 0, 0)
            count = count + jnp.where(jnp.logical_and(in_ring, z == 0), 7, 0)
        else:
            greet_ring(jnp.logical_or(z == 2, z == 6), 0)
            greet_ring(jnp.logical_or(z == 1, jnp.logical_or(z == 3, z == 4)), 2)
            greet_ring(jnp.logical_or(z == 5, z == 7), 6)
            fan = jnp.where(z == 2, 3, jnp.where(jnp.logical_or(z == 0, z == 6), 2, 0))
            count = count + jnp.where(in_ring, fan, 0)

    pl.semaphore_wait(barrier, count)

    def remote(src, dst, send, recv, target):
        return pltpu.make_async_remote_copy(
            src_ref=src, dst_ref=dst, send_sem=send, recv_sem=recv, device_id=target,
            device_id_type=MESH,
        )

    corner_src = a_ref.at[0:TILE, 0:TILE]

    def corner_z(tile):
        mine = jnp.logical_and(jnp.logical_and(x == root_x[tile], y == 0), k == root_core[tile])

        @pl.when(jnp.logical_and(mine, z == 0))
        def _():
            targets = Z_FAN[0] if tile else tuple(range(1, RING_Z))
            for i, to in enumerate(targets):
                remote(
                    corner_src, cn.at[tile], cn_send.at[tile, i],
                    cn_recv.at[tile], (root_x[tile], to * 2 + root_core[tile]),
                ).start()
            pltpu.make_async_copy(corner_src, cn.at[tile], cn_recv.at[tile]).start()

    def corner_wait(tile):
        pltpu.make_async_copy(corner_src, cn.at[tile], cn_recv.at[tile]).wait()

    def corner_send(tile, sem, target):
        remote(cn.at[tile], cn.at[tile], cn_send.at[tile, sem], cn_recv.at[tile], target).start()

    def corner_x(tile):
        mine = jnp.logical_and(jnp.logical_and(x == root_x[tile], y == 0), k == root_core[tile])

        @pl.when(mine)
        def _():
            corner_wait(tile)
            if tile:
                for place_z in (2, 6):

                    @pl.when(z == place_z)
                    def _(place_z=place_z):
                        for i, to in enumerate(Z_FAN[place_z]):
                            corner_send(tile, i, (root_x[tile], to * 2 + root_core[tile]))

            corner_send(tile, 7, around[0])
            corner_send(tile, 8, around[2])
            corner_send(tile, 9, x_far)
            corner_send(tile, 10, around[1])
            corner_send(tile, 11, around[3])
            corner_send(tile, 12, y_far)
            remote(cn.at[tile], cn.at[tile], cn_sib.at[tile], cn_recv.at[tile], sibling).start()

    def corner_y(tile):
        mine = jnp.logical_and(k == root_core[tile], jnp.logical_and(y == 0, x != root_x[tile]))

        @pl.when(mine)
        def _():
            corner_wait(tile)
            corner_send(tile, 10, around[1])
            corner_send(tile, 11, around[3])
            corner_send(tile, 12, y_far)
            remote(cn.at[tile], cn.at[tile], cn_sib.at[tile], cn_recv.at[tile], sibling).start()

    def corner_end(tile):
        @pl.when(jnp.logical_and(k == root_core[tile], y != 0))
        def _():
            corner_wait(tile)
            remote(cn.at[tile], cn.at[tile], cn_sib.at[tile], cn_recv.at[tile], sibling).start()

        @pl.when(k != root_core[tile])
        def _():
            corner_wait(tile)

    def corner_drain(tile):
        mine = k == root_core[tile]
        here = cn.at[tile]

        def sent(sem):
            remote(here, here, sem, cn_recv.at[tile], sibling).wait_send()

        @pl.when(mine)
        def _():
            sent(cn_sib.at[tile])

            @pl.when(y == 0)
            def _():
                for i in (10, 11, 12):
                    sent(cn_send.at[tile, i])

            @pl.when(jnp.logical_and(y == 0, x == root_x[tile]))
            def _():
                for i in (7, 8, 9):
                    sent(cn_send.at[tile, i])

                for place_z in (0, 2, 6) if tile else (0,):

                    @pl.when(z == place_z)
                    def _(place_z=place_z):
                        for i in range(len(Z_FAN[place_z]) if tile else 7):
                            sent(cn_send.at[tile, i])

    def z_rows(j):
        return pl.ds(j * ZROWS, ZROWS)

    def z_send_chunk(j, way, src, target):
        remote(src, hr.at[k, z_rows(j)], z_send.at[way], z_recv.at[j], target).start()

    def z_sibling(j, src):
        remote(src, hr.at[k, z_rows(j)], z_sib_send, z_sib_recv.at[j], sibling).start()

    def z_service(j, place_here):
        @pl.when(pos == place_here)
        def _():
            here = hr.at[k, z_rows(j)]
            pltpu.make_async_copy(here, here, z_recv.at[j]).wait()
            if place_here in (1, 2, 4):
                z_send_chunk(j, 0, here, z_next)
            if place_here == 2:
                z_send_chunk(j, 1, here, z_skip)
            if place_here == 7:
                z_send_chunk(j, 0, here, z_prev)
            z_sibling(j, here)

    whole_r = hr.at[k]

    def z_sent(way):
        remote(whole_r, whole_r, z_send.at[way], z_sib_recv.at[0], sibling).wait_send()

    trees = []
    for s in range(2):
        for d in range(4):
            fx, fy = wrap(x - s + RING_X, RING_X), y
            for _ in range(d):
                fx, fy = fy, wrap(RING_X - fx, RING_X)
            at = fx + RING_X * fy
            trees.append((s, d, at))

    def p_rows(d, j):
        start = d * (TILE // 4) + j * PROWS
        return slice(start, start + PROWS)

    def among(at, spots):
        found = at == spots[0][0] + RING_X * spots[0][1]
        for spot in spots[1:]:
            found = jnp.logical_or(found, at == spot[0] + RING_X * spot[1])
        return found

    def p_service(index, j, level):
        s, d, at = trees[index]
        here = hc.at[s, p_rows(d, j)]
        spots = [spot for spot in TREE if LEVEL[spot] == level]

        @pl.when(among(at, spots))
        def _():
            if level == 0:
                src = a_ref.at[p_rows(d, j)]
            else:
                src = here
                pltpu.make_async_copy(here, here, p_recv.at[index, j]).wait()
            for way in range(5):
                users = [spot for spot in spots if way in TREE[spot]]
                if users:

                    def send(way=way):
                        remote(
                            src, here, p_send.at[index, way], p_recv.at[index, j],
                            corners[d] if way == 4 else around[(way + d) % 4],
                        ).start()

                    if len(users) == len(spots):
                        send()
                    else:
                        pl.when(among(at, users))(send)

    def p_end(index):
        s, d, at = trees[index]

        @pl.when(jnp.logical_not(among(at, list(TREE))))
        def _():
            for j in range(PCH):
                here = hc.at[s, p_rows(d, j)]
                pltpu.make_async_copy(here, here, p_recv.at[index, j]).wait()

    def p_drain(index):
        s, d, at = trees[index]
        part = hc.at[s, d * (TILE // 4) : (d + 1) * (TILE // 4)]

        @pl.when(among(at, list(TREE)))
        def _():
            for way in range(5):

                @pl.when(among(at, [spot for spot in TREE if way in TREE[spot]]))
                def _(way=way):
                    remote(
                        part, part, p_send.at[index, way], p_recv.at[index, 0], sibling
                    ).wait_send()

    for tile in range(3):
        corner_z(tile)

    @pl.when(pos == 0)
    def _():
        for j in range(ZCH):
            z_send_chunk(j, 0, a_ref.at[z_rows(j), 0:TILE], z_next)
        for j in range(ZCH):
            z_sibling(j, a_ref.at[z_rows(j), 0:TILE])
        pltpu.make_async_copy(a_ref.at[:, 0:TILE], hr.at[k], z_own).start()

    for j in range(PCH):
        for index in range(8):
            p_service(index, j, 0)

    @pl.when(r < 2)
    def _():
        pltpu.make_async_copy(a_ref.at[0:TILE, :], hc.at[r], p_own).start()

    def second_wave():
        @pl.when(pos == 0)
        def _():
            z_sent(0)
            for j in range(ZCH):
                z_send_chunk(j, 1, a_ref.at[z_rows(j), 0:TILE], z_prev)

    z_level = {1: 0, 2: 1, 3: 2, 4: 2, 5: 3, 7: 3, 6: 4}
    def slot_work(slot):
        if slot in CX:
            for tile in CX[slot]:
                corner_x(tile)
        if slot == 7:
            second_wave()
        if slot in CY:
            for tile in CY[slot]:
                corner_y(tile)
        for j in range(ZCH):
            for where_, level in ((1, 1), (2, 2), (3, 3), (4, 3), (5, 4)):
                if HOP * level + j * 8 // ZCH == slot:
                    z_service(j, where_)
            for where_, level in ((7, 1), (6, 2)):
                if 8 + HOP * level + j * 8 // ZCH == slot:
                    z_service(j, where_)
        for j in range(PCH):
            for level in range(1, 4):
                if HOP * level + 2 * j == slot:
                    for index in range(8):
                        p_service(index, j, level)

    def chain():
        corner_end(0)
        w0 = yield from cholesky_inverse(cn[0])
        w_all[:TILE, :TILE] = w0
        w_all[:TILE, TILE:] = jnp.zeros((TILE, TILE), jnp.float32)
        corner_end(1)
        corner_end(2)
        u01 = dot(w0, cn[1], ((1,), (1,)))
        w_all[TILE:, :TILE] = dot(u01, w0, ((0,), (0,)))
        yield
        w1 = yield from cholesky_inverse(cn[2] - dot(u01, u01, ((0,), (0,))))
        w_all[TILE:, TILE:] = w1
        w_all[TILE:, :TILE] = -dot(w1, w_all[TILE:, :TILE], ((1,), (0,)))

    def columns():
        @pl.when(r < 2)
        def _():
            pltpu.make_async_copy(a_ref.at[0:TILE, :], hc.at[r], p_own).wait()

        for index in range(8):
            p_end(index)
        for i in range(SIDE // 256):
            lanes = slice(i * 256, i * 256 + 256)
            raw = jnp.concatenate([hc[0, :, lanes], hc[1, :, lanes]], axis=0)
            got = panel_dot(w_all[...], raw, ((1,), (0,)))
            high = got.astype(jnp.bfloat16)
            pc_hi_ref[:, lanes] = high
            pc_lo_ref[:, lanes] = (got - high.astype(jnp.float32)).astype(jnp.bfloat16)

        @pl.when(pos == 0)
        def _():
            pltpu.make_async_copy(a_ref.at[:, 0:TILE], hr.at[k], z_own).wait()

        pltpu.make_async_copy(a_ref, a_out, a_sem).wait()

    def rows_done():
        for j in range(ZCH):
            other = hr.at[1 - k, z_rows(j)]
            pltpu.make_async_copy(other, other, z_sib_recv.at[j]).wait()
        for i in range(SIDE // 256):
            rows = slice(i * 256, i * 256 + 256)
            raw = jnp.concatenate([hr[0, rows], hr[1, rows]], axis=1)
            pr_ref[rows] = panel_dot(raw, w_all[...], ((1,), (1,)))

    def work():
        yield from chain()
        yield
        while len(slots_seen) < PC_SLOT:
            yield
        columns()
        yield
        while len(slots_seen) < 50:
            yield
        rows_done()

    slots_seen = []
    steps = work()
    for slot in range(1, 23):
        slots_seen.append(slot)
        slot_work(slot)
        if slot >= FIRST:
            for _ in range(PER_SLOT):
                next(steps, None)
    slots_seen.extend(range(100))
    for _ in steps:
        pass

    for tile in range(3):
        corner_drain(tile)
    remote(whole_r, whole_r, z_sib_send, z_sib_recv.at[0], sibling).wait_send()

    @pl.when(jnp.logical_or(jnp.logical_or(pos == 1, pos == 2), jnp.logical_or(pos == 4, pos == 7)))
    def _():
        z_sent(0)

    @pl.when(jnp.logical_or(pos == 0, pos == 2))
    def _():
        z_sent(1)

    for index in range(8):
        p_drain(index)


def panels(matrix):
    vmem = pl.BlockSpec(memory_space=pltpu.VMEM)
    f32 = jnp.float32
    dma = pltpu.SemaphoreType.DMA
    return pl.pallas_call(
        panels_kernel,
        out_shape=[
            pltpu.VMEM((SIDE, SIDE), f32),
            pltpu.VMEM((SIDE, 2 * TILE), f32),
            pltpu.VMEM((2 * TILE, SIDE), jnp.bfloat16),
            pltpu.VMEM((2 * TILE, SIDE), jnp.bfloat16),
        ],
        in_specs=[pl.BlockSpec(memory_space=pl.ANY)],
        out_specs=[vmem] * 4,
        scratch_shapes=[
            pltpu.VMEM((2, SIDE, TILE), f32),
            pltpu.VMEM((2, TILE, SIDE), f32),
            pltpu.VMEM((3, TILE, TILE), f32),
            pltpu.VMEM((2 * TILE, 2 * TILE), f32),
            dma((3,)), dma((3, 13)), dma((3,)),
            dma((ZCH,)), dma((2,)), dma((ZCH,)), dma, dma,
            dma((8, PCH)), dma((8, 5)), dma, dma,
        ],
        compiler_params=pltpu.CompilerParams(
            collective_id=0, has_side_effects=True, vmem_limit_bytes=VMEM_LIMIT
        ),
        name="panels",
    )(matrix)


def finished(i, raw, panel, pc_hi_ref, pc_lo_ref):
    r = lax.axis_index("row")
    c = lax.axis_index("col")

    def part(left, right):
        return lax.dot_general(
            left, right[...], (((1,), (0,)), ((), ())), preferred_element_type=jnp.float32
        )

    high = panel.astype(jnp.bfloat16)
    low = (panel - high.astype(jnp.float32)).astype(jnp.bfloat16)
    full = raw - (part(high, pc_hi_ref) + (part(high, pc_lo_ref) + part(low, pc_hi_ref)))
    first = jnp.where(c == 0, panel[:, :TILE], jnp.where(c == 1, panel[:, TILE:], full[:, :TILE]))
    wide = full[:, TILE:]
    if i == 0:
        row = lax.broadcasted_iota(jnp.int32, (TILE, TILE), 0)
        lane = lax.broadcasted_iota(jnp.int32, (TILE, TILE), 1)
        kept = jnp.logical_or(c < r, jnp.logical_and(c == r, lane <= row))
        first = jnp.where(jnp.logical_and(r < 2, jnp.logical_not(kept)), 0.0, first)
        wide = jnp.where(r < 2, 0.0, wide)
    return first, wide


def finish_kernel(a_ref, pr_ref, pc_hi_ref, pc_lo_ref, out_ref, stage, sem):
    copies = []
    for i in range(SIDE // TILE):
        rows = slice(i * TILE, (i + 1) * TILE)
        first, wide = finished(i, a_ref[rows], pr_ref[rows], pc_hi_ref, pc_lo_ref)
        stage[rows, :TILE] = first
        stage[rows, TILE:] = wide
        copies.append(pltpu.make_async_copy(stage.at[rows], out_ref.at[rows], sem.at[i]))
        copies[-1].start()
    for copy in copies:
        copy.wait()


def finish(a, pr, pc_hi, pc_lo):
    vmem = pl.BlockSpec(memory_space=pltpu.VMEM)
    return pl.pallas_call(
        finish_kernel,
        out_shape=jax.ShapeDtypeStruct((SIDE, SIDE), jnp.float32),
        in_specs=[vmem] * 4,
        out_specs=pl.BlockSpec(memory_space=pl.ANY),
        scratch_shapes=[
            pltpu.VMEM((SIDE, SIDE), jnp.float32), pltpu.SemaphoreType.DMA((SIDE // TILE,)),
        ],
        compiler_params=pltpu.CompilerParams(vmem_limit_bytes=UPDATE_LIMIT),
        name="finish",
    )(a, pr, pc_hi, pc_lo)


def per_device(matrix):
    return finish(*panels(matrix))


def solution(mesh):
    return jax.shard_map(
        per_device, mesh=mesh, in_specs=(P("row", "col"),), out_specs=P("row", "col"),
        check_vma=False,
    )
```

```python
import functools

import jax
import jax.numpy as jnp
from jax import lax
from jax.experimental import pallas as pl
from jax.experimental.pallas import tpu as pltpu
from jax.sharding import PartitionSpec as P

TILE = 128
SUP = 64
SIDE = 1280
RING_X = 4
RING_Y = 4
RING_Z = 8
ZCH = 16
ZROWS = SIDE // ZCH
PCH = 4
PROWS = TILE // 4 // PCH
FIRST = 10
CX = {4: (0,), 7: (1, 2)}
CY = {8: (0,), 11: (1, 2)}
PC_SLOT = 20
PER_SLOT = 4
VMEM_LIMIT = 40 * 2**20
UPDATE_LIMIT = 24 * 2**20
EXACT = lax.Precision.HIGHEST
MESH = pl.DeviceIdType.MESH


def dot(left, right, dims):
    return lax.dot_general(
        left, right, (dims, ((), ())), precision=EXACT, preferred_element_type=jnp.float32
    )


def panel_dot(left, right, dims):
    def split(value):
        high = value.astype(jnp.bfloat16)
        return high, (value - high.astype(jnp.float32)).astype(jnp.bfloat16)

    def part(a, b):
        return lax.dot_general(a, b, (dims, ((), ())), preferred_element_type=jnp.float32)

    left_high, left_low = split(left)
    right_high, right_low = split(right)
    return part(left_high, right_high) + (part(left_high, right_low) + part(left_low, right_high))


def cholesky_inverse(tile):
    sub = lax.broadcasted_iota(jnp.int32, (8, TILE), 0)
    lane = lax.broadcasted_iota(jnp.int32, (8, TILE), 1)
    count = TILE // 8
    a = [tile[8 * i : 8 * i + 8] for i in range(count)]
    w = [jnp.where(lane == sub + 8 * i, 1.0, 0.0) for i in range(count)]
    for start in range(0, TILE, SUP):
        blocks = list(range(start // 8, (start + SUP) // 8))
        for t in blocks:
            j0 = 8 * t
            rest = [m for m in blocks if m >= t]
            col = {
                m: [jnp.broadcast_to(a[m][:, j0 + q : j0 + q + 1], (8, TILE)) for q in range(8)]
                for m in rest
            }
            scale = jnp.zeros((8, TILE), jnp.float32)
            for p in range(8):
                root = lax.rsqrt(jnp.broadcast_to(col[t][p][p : p + 1], (8, TILE)))
                scale = jnp.where(sub == p, root, scale)
                row_a = jnp.broadcast_to(a[t][p : p + 1], (8, TILE)) * root
                row_w = jnp.broadcast_to(w[t][p : p + 1], (8, TILE)) * root
                piece = {
                    q: jnp.broadcast_to(col[t][q][p : p + 1], (8, TILE)) * root
                    for q in range(p + 1, 8)
                }
                for m in rest:
                    factor = col[m][p] * root
                    for q in range(p + 1, 8):
                        col[m][q] = col[m][q] - factor * piece[q]
                    if m == t:
                        factor = jnp.where(sub > p, factor, 0.0)
                    a[m] = a[m] - factor * row_a
                    w[m] = w[m] - factor * row_w
            a[t] = a[t] * scale
            w[t] = w[t] * scale
            yield
        end = start + SUP
        if end < TILE:
            upper = jnp.concatenate([a[m] for m in blocks], 0)
            both = jnp.concatenate([upper, jnp.concatenate([w[m] for m in blocks], 0)], 1)
            change = dot(upper, both, ((0,), (0,)))
            for m in range(end // 8, count):
                a[m] = a[m] - change[8 * m : 8 * m + 8, :TILE]
                w[m] = w[m] - change[8 * m : 8 * m + 8, TILE:]
            yield
    return jnp.concatenate(w, 0)


def place():
    r = lax.axis_index("row")
    c = lax.axis_index("col")
    return r % RING_X, r // RING_X, c // 2, c % 2


def device(x, y, z, k):
    return (y * RING_X + x, z * 2 + k)


def wrap(i, n):
    return lax.rem(i + n, n)


TREE = {
    (0, 0): (0,), (1, 0): (0, 1, 3), (2, 0): (0, 3), (1, 1): (0, 1, 2), (1, 3): (2,),
    (2, 1): (0, 1, 4), (2, 3): (0,), (1, 2): (2,),
}
LEVEL = {(0, 0): 0, (1, 0): 1, (2, 0): 2, (1, 1): 2, (1, 3): 2, (2, 1): 3, (2, 3): 3, (1, 2): 3}
STEPS = ((1, 0), (0, 1), (-1, 0), (0, -1))
HOP = 3
WAVE = 9
Z_FAN = {0: (2, 6), 2: (1, 3, 4), 6: (5, 7)}


def panels_kernel(
    a_ref, a_out, pr_ref, pc_hi_ref, pc_lo_ref,
    hr, hc, cn, w_all,
    cn_recv, cn_send, cn_sib, z_recv, z_send, z_sib_recv, z_sib_send, z_own,
    p_recv, p_send, p_own, a_sem,
):
    x, y, z, k = place()
    r = y * RING_X + x
    sibling = device(x, y, z, 1 - k)
    step = 1 - 2 * k
    pos = jnp.where(k == 0, z, wrap(RING_Z - z, RING_Z))
    around = (
        device(wrap(x + 1, RING_X), y, z, k),
        device(x, wrap(y + 1, RING_Y), z, k),
        device(wrap(x - 1, RING_X), y, z, k),
        device(x, wrap(y - 1, RING_Y), z, k),
    )
    corners = tuple(
        device(wrap(x + dx, RING_X), wrap(y + dy, RING_Y), z, k)
        for dx, dy in ((1, 1), (-1, 1), (-1, -1), (1, -1))
    )
    z_next = device(x, y, wrap(z + step, RING_Z), k)
    z_prev = device(x, y, wrap(z - step, RING_Z), k)
    z_skip = device(x, y, wrap(z + 2 * step, RING_Z), k)
    z_back = device(x, y, wrap(z - 2 * step, RING_Z), k)
    x_far = device(wrap(x + 2, RING_X), y, z, k)
    y_far = device(x, wrap(y + 2, RING_Y), z, k)

    pltpu.make_async_copy(a_ref, a_out, a_sem).start()
    barrier = pltpu.get_barrier_semaphore()

    def greet(target):
        pl.semaphore_signal(barrier, inc=1, device_id=target, device_id_type=MESH)

    for target in (sibling, z_next, z_prev, x_far, y_far) + around + corners:
        greet(target)

    @pl.when(pos == 4)
    def _():
        greet(z_back)

    root_core = (0, 0, 1)
    root_x = (0, 1, 1)
    count = 13 + jnp.where(pos == 2, 1, 0)
    for tile in range(3):
        in_ring = jnp.logical_and(jnp.logical_and(x == root_x[tile], y == 0), k == root_core[tile])

        def greet_ring(where_, place_z, tile=tile, in_ring=in_ring):
            @pl.when(jnp.logical_and(in_ring, where_))
            def _():
                greet((root_x[tile], place_z * 2 + root_core[tile]))

        if tile == 0:
            greet_ring(z != 0, 0)
            count = count + jnp.where(jnp.logical_and(in_ring, z == 0), 7, 0)
        else:
            greet_ring(jnp.logical_or(z == 2, z == 6), 0)
            greet_ring(jnp.logical_or(z == 1, jnp.logical_or(z == 3, z == 4)), 2)
            greet_ring(jnp.logical_or(z == 5, z == 7), 6)
            fan = jnp.where(z == 2, 3, jnp.where(jnp.logical_or(z == 0, z == 6), 2, 0))
            count = count + jnp.where(in_ring, fan, 0)

    pl.semaphore_wait(barrier, count)

    def remote(src, dst, send, recv, target):
        return pltpu.make_async_remote_copy(
            src_ref=src, dst_ref=dst, send_sem=send, recv_sem=recv, device_id=target,
            device_id_type=MESH,
        )

    corner_src = a_ref.at[0:TILE, 0:TILE]

    def corner_z(tile):
        mine = jnp.logical_and(jnp.logical_and(x == root_x[tile], y == 0), k == root_core[tile])

        @pl.when(jnp.logical_and(mine, z == 0))
        def _():
            targets = Z_FAN[0] if tile else tuple(range(1, RING_Z))
            for i, to in enumerate(targets):
                remote(
                    corner_src, cn.at[tile], cn_send.at[tile, i],
                    cn_recv.at[tile], (root_x[tile], to * 2 + root_core[tile]),
                ).start()
            pltpu.make_async_copy(corner_src, cn.at[tile], cn_recv.at[tile]).start()

    def corner_wait(tile):
        pltpu.make_async_copy(corner_src, cn.at[tile], cn_recv.at[tile]).wait()

    def corner_send(tile, sem, target):
        remote(cn.at[tile], cn.at[tile], cn_send.at[tile, sem], cn_recv.at[tile], target).start()

    def corner_x(tile):
        mine = jnp.logical_and(jnp.logical_and(x == root_x[tile], y == 0), k == root_core[tile])

        @pl.when(mine)
        def _():
            corner_wait(tile)
            if tile:
                for place_z in (2, 6):

                    @pl.when(z == place_z)
                    def _(place_z=place_z):
                        for i, to in enumerate(Z_FAN[place_z]):
                            corner_send(tile, i, (root_x[tile], to * 2 + root_core[tile]))

            corner_send(tile, 7, around[0])
            corner_send(tile, 8, around[2])
            corner_send(tile, 9, x_far)
            corner_send(tile, 10, around[1])
            corner_send(tile, 11, around[3])
            corner_send(tile, 12, y_far)
            remote(cn.at[tile], cn.at[tile], cn_sib.at[tile], cn_recv.at[tile], sibling).start()

    def corner_y(tile):
        mine = jnp.logical_and(k == root_core[tile], jnp.logical_and(y == 0, x != root_x[tile]))

        @pl.when(mine)
        def _():
            corner_wait(tile)
            corner_send(tile, 10, around[1])
            corner_send(tile, 11, around[3])
            corner_send(tile, 12, y_far)
            remote(cn.at[tile], cn.at[tile], cn_sib.at[tile], cn_recv.at[tile], sibling).start()

    def corner_end(tile):
        @pl.when(jnp.logical_and(k == root_core[tile], y != 0))
        def _():
            corner_wait(tile)
            remote(cn.at[tile], cn.at[tile], cn_sib.at[tile], cn_recv.at[tile], sibling).start()

        @pl.when(k != root_core[tile])
        def _():
            corner_wait(tile)

    def corner_drain(tile):
        mine = k == root_core[tile]
        here = cn.at[tile]

        def sent(sem):
            remote(here, here, sem, cn_recv.at[tile], sibling).wait_send()

        @pl.when(mine)
        def _():
            sent(cn_sib.at[tile])

            @pl.when(y == 0)
            def _():
                for i in (10, 11, 12):
                    sent(cn_send.at[tile, i])

            @pl.when(jnp.logical_and(y == 0, x == root_x[tile]))
            def _():
                for i in (7, 8, 9):
                    sent(cn_send.at[tile, i])

                for place_z in (0, 2, 6) if tile else (0,):

                    @pl.when(z == place_z)
                    def _(place_z=place_z):
                        for i in range(len(Z_FAN[place_z]) if tile else 7):
                            sent(cn_send.at[tile, i])

    def z_rows(j):
        return pl.ds(j * ZROWS, ZROWS)

    def z_send_chunk(j, way, src, target):
        remote(src, hr.at[k, z_rows(j)], z_send.at[way], z_recv.at[j], target).start()

    def z_sibling(j, src):
        remote(src, hr.at[k, z_rows(j)], z_sib_send, z_sib_recv.at[j], sibling).start()

    def z_service(j, place_here):
        @pl.when(pos == place_here)
        def _():
            here = hr.at[k, z_rows(j)]
            pltpu.make_async_copy(here, here, z_recv.at[j]).wait()
            if place_here in (1, 2, 4):
                z_send_chunk(j, 0, here, z_next)
            if place_here == 2:
                z_send_chunk(j, 1, here, z_skip)
            if place_here == 7:
                z_send_chunk(j, 0, here, z_prev)
            z_sibling(j, here)

    whole_r = hr.at[k]

    def z_sent(way):
        remote(whole_r, whole_r, z_send.at[way], z_sib_recv.at[0], sibling).wait_send()

    trees = []
    for s in range(2):
        for d in range(4):
            fx, fy = wrap(x - s + RING_X, RING_X), y
            for _ in range(d):
                fx, fy = fy, wrap(RING_X - fx, RING_X)
            at = fx + RING_X * fy
            trees.append((s, d, at))

    def p_rows(d, j):
        start = d * (TILE // 4) + j * PROWS
        return slice(start, start + PROWS)

    def among(at, spots):
        found = at == spots[0][0] + RING_X * spots[0][1]
        for spot in spots[1:]:
            found = jnp.logical_or(found, at == spot[0] + RING_X * spot[1])
        return found

    def p_service(index, j, level):
        s, d, at = trees[index]
        here = hc.at[s, p_rows(d, j)]
        spots = [spot for spot in TREE if LEVEL[spot] == level]

        @pl.when(among(at, spots))
        def _():
            if level == 0:
                src = a_ref.at[p_rows(d, j)]
            else:
                src = here
                pltpu.make_async_copy(here, here, p_recv.at[index, j]).wait()
            for way in range(5):
                users = [spot for spot in spots if way in TREE[spot]]
                if users:

                    def send(way=way):
                        remote(
                            src, here, p_send.at[index, way], p_recv.at[index, j],
                            corners[d] if way == 4 else around[(way + d) % 4],
                        ).start()

                    if len(users) == len(spots):
                        send()
                    else:
                        pl.when(among(at, users))(send)

    def p_end(index):
        s, d, at = trees[index]

        @pl.when(jnp.logical_not(among(at, list(TREE))))
        def _():
            for j in range(PCH):
                here = hc.at[s, p_rows(d, j)]
                pltpu.make_async_copy(here, here, p_recv.at[index, j]).wait()

    def p_drain(index):
        s, d, at = trees[index]
        part = hc.at[s, d * (TILE // 4) : (d + 1) * (TILE // 4)]

        @pl.when(among(at, list(TREE)))
        def _():
            for way in range(5):

                @pl.when(among(at, [spot for spot in TREE if way in TREE[spot]]))
                def _(way=way):
                    remote(
                        part, part, p_send.at[index, way], p_recv.at[index, 0], sibling
                    ).wait_send()

    for tile in range(3):
        corner_z(tile)

    @pl.when(pos == 0)
    def _():
        for j in range(ZCH):
            z_send_chunk(j, 0, a_ref.at[z_rows(j), 0:TILE], z_next)
        for j in range(ZCH):
            z_sibling(j, a_ref.at[z_rows(j), 0:TILE])
        pltpu.make_async_copy(a_ref.at[:, 0:TILE], hr.at[k], z_own).start()

    for j in range(PCH):
        for index in range(8):
            p_service(index, j, 0)

    @pl.when(r < 2)
    def _():
        pltpu.make_async_copy(a_ref.at[0:TILE, :], hc.at[r], p_own).start()

    def second_wave():
        @pl.when(pos == 0)
        def _():
            z_sent(0)
            for j in range(ZCH):
                z_send_chunk(j, 1, a_ref.at[z_rows(j), 0:TILE], z_prev)

    z_level = {1: 0, 2: 1, 3: 2, 4: 2, 5: 3, 7: 3, 6: 4}
    def slot_work(slot):
        if slot in CX:
            for tile in CX[slot]:
                corner_x(tile)
        if slot == WAVE:
            second_wave()
        if slot in CY:
            for tile in CY[slot]:
                corner_y(tile)
        for j in range(ZCH):
            for where_, level in ((1, 1), (2, 2), (3, 3), (4, 3), (5, 4)):
                if HOP * level + j * 8 // ZCH == slot:
                    z_service(j, where_)
            for where_, level in ((7, 1), (6, 2)):
                if WAVE + 1 + HOP * level + j * 8 // ZCH == slot:
                    z_service(j, where_)
        for j in range(PCH):
            for level in range(1, 4):
                if HOP * level + 2 * j == slot:
                    for index in range(8):
                        p_service(index, j, level)

    def chain():
        corner_end(0)
        w0 = yield from cholesky_inverse(cn[0])
        w_all[:TILE, :TILE] = w0
        w_all[:TILE, TILE:] = jnp.zeros((TILE, TILE), jnp.float32)
        corner_end(1)
        corner_end(2)
        u01 = dot(w0, cn[1], ((1,), (1,)))
        w_all[TILE:, :TILE] = dot(u01, w0, ((0,), (0,)))
        yield
        w1 = yield from cholesky_inverse(cn[2] - dot(u01, u01, ((0,), (0,))))
        w_all[TILE:, TILE:] = w1
        w_all[TILE:, :TILE] = -dot(w1, w_all[TILE:, :TILE], ((1,), (0,)))

    def columns():
        @pl.when(r < 2)
        def _():
            pltpu.make_async_copy(a_ref.at[0:TILE, :], hc.at[r], p_own).wait()

        for index in range(8):
            p_end(index)
        for i in range(SIDE // 256):
            lanes = slice(i * 256, i * 256 + 256)
            raw = jnp.concatenate([hc[0, :, lanes], hc[1, :, lanes]], axis=0)
            got = panel_dot(w_all[...], raw, ((1,), (0,)))
            high = got.astype(jnp.bfloat16)
            pc_hi_ref[:, lanes] = high
            pc_lo_ref[:, lanes] = (got - high.astype(jnp.float32)).astype(jnp.bfloat16)

        @pl.when(pos == 0)
        def _():
            pltpu.make_async_copy(a_ref.at[:, 0:TILE], hr.at[k], z_own).wait()

        pltpu.make_async_copy(a_ref, a_out, a_sem).wait()

    def rows_done():
        for j in range(ZCH):
            other = hr.at[1 - k, z_rows(j)]
            pltpu.make_async_copy(other, other, z_sib_recv.at[j]).wait()
        for i in range(SIDE // 256):
            rows = slice(i * 256, i * 256 + 256)
            raw = jnp.concatenate([hr[0, rows], hr[1, rows]], axis=1)
            pr_ref[rows] = panel_dot(raw, w_all[...], ((1,), (1,)))

    def work():
        yield from chain()
        yield
        while len(slots_seen) < PC_SLOT:
            yield
        columns()
        yield
        while len(slots_seen) < 50:
            yield
        for tile in range(3):
            corner_drain(tile)
        for index in range(8):
            p_drain(index)
        rows_done()

    slots_seen = []
    steps = work()
    for slot in range(1, WAVE + 16):
        slots_seen.append(slot)
        slot_work(slot)
        if slot >= FIRST:
            for _ in range(PER_SLOT):
                next(steps, None)
    slots_seen.extend(range(100))
    for _ in steps:
        pass

    remote(whole_r, whole_r, z_sib_send, z_sib_recv.at[0], sibling).wait_send()

    @pl.when(jnp.logical_or(jnp.logical_or(pos == 1, pos == 2), jnp.logical_or(pos == 4, pos == 7)))
    def _():
        z_sent(0)

    @pl.when(jnp.logical_or(pos == 0, pos == 2))
    def _():
        z_sent(1)


def panels(matrix):
    vmem = pl.BlockSpec(memory_space=pltpu.VMEM)
    f32 = jnp.float32
    dma = pltpu.SemaphoreType.DMA
    return pl.pallas_call(
        panels_kernel,
        out_shape=[
            pltpu.VMEM((SIDE, SIDE), f32),
            pltpu.VMEM((SIDE, 2 * TILE), f32),
            pltpu.VMEM((2 * TILE, SIDE), jnp.bfloat16),
            pltpu.VMEM((2 * TILE, SIDE), jnp.bfloat16),
        ],
        in_specs=[pl.BlockSpec(memory_space=pl.ANY)],
        out_specs=[vmem] * 4,
        scratch_shapes=[
            pltpu.VMEM((2, SIDE, TILE), f32),
            pltpu.VMEM((2, TILE, SIDE), f32),
            pltpu.VMEM((3, TILE, TILE), f32),
            pltpu.VMEM((2 * TILE, 2 * TILE), f32),
            dma((3,)), dma((3, 13)), dma((3,)),
            dma((ZCH,)), dma((2,)), dma((ZCH,)), dma, dma,
            dma((8, PCH)), dma((8, 5)), dma, dma,
        ],
        compiler_params=pltpu.CompilerParams(
            collective_id=0, has_side_effects=True, vmem_limit_bytes=VMEM_LIMIT
        ),
        name="panels",
    )(matrix)


def finished(i, raw, panel, pc_hi_ref, pc_lo_ref):
    r = lax.axis_index("row")
    c = lax.axis_index("col")

    def part(left, right):
        return lax.dot_general(
            left, right[...], (((1,), (0,)), ((), ())), preferred_element_type=jnp.float32
        )

    high = panel.astype(jnp.bfloat16)
    low = (panel - high.astype(jnp.float32)).astype(jnp.bfloat16)
    full = raw - (part(high, pc_hi_ref) + (part(high, pc_lo_ref) + part(low, pc_hi_ref)))
    first = jnp.where(c == 0, panel[:, :TILE], jnp.where(c == 1, panel[:, TILE:], full[:, :TILE]))
    wide = full[:, TILE:]
    if i == 0:
        row = lax.broadcasted_iota(jnp.int32, (TILE, TILE), 0)
        lane = lax.broadcasted_iota(jnp.int32, (TILE, TILE), 1)
        kept = jnp.logical_or(c < r, jnp.logical_and(c == r, lane <= row))
        first = jnp.where(jnp.logical_and(r < 2, jnp.logical_not(kept)), 0.0, first)
        wide = jnp.where(r < 2, 0.0, wide)
    return first, wide


def finish_kernel(a_ref, pr_ref, pc_hi_ref, pc_lo_ref, out_ref, stage, sem):
    copies = []
    for i in range(SIDE // TILE):
        rows = slice(i * TILE, (i + 1) * TILE)
        first, wide = finished(i, a_ref[rows], pr_ref[rows], pc_hi_ref, pc_lo_ref)
        stage[rows, :TILE] = first
        stage[rows, TILE:] = wide
        copies.append(pltpu.make_async_copy(stage.at[rows], out_ref.at[rows], sem.at[i]))
        copies[-1].start()
    for copy in copies:
        copy.wait()


def finish(a, pr, pc_hi, pc_lo):
    vmem = pl.BlockSpec(memory_space=pltpu.VMEM)
    return pl.pallas_call(
        finish_kernel,
        out_shape=jax.ShapeDtypeStruct((SIDE, SIDE), jnp.float32),
        in_specs=[vmem] * 4,
        out_specs=pl.BlockSpec(memory_space=pl.ANY),
        scratch_shapes=[
            pltpu.VMEM((SIDE, SIDE), jnp.float32), pltpu.SemaphoreType.DMA((SIDE // TILE,)),
        ],
        compiler_params=pltpu.CompilerParams(vmem_limit_bytes=UPDATE_LIMIT),
        name="finish",
    )(a, pr, pc_hi, pc_lo)


def per_device(matrix):
    return finish(*panels(matrix))


def solution(mesh):
    return jax.shard_map(
        per_device, mesh=mesh, in_specs=(P("row", "col"),), out_specs=P("row", "col"),
        check_vma=False,
    )
```

```python
import functools

import jax
import jax.numpy as jnp
from jax import lax
from jax.experimental import pallas as pl
from jax.experimental.pallas import tpu as pltpu
from jax.sharding import PartitionSpec as P

TILE = 128
SUP = 64
SIDE = 1280
RING_X = 4
RING_Y = 4
RING_Z = 8
ZCH = 16
ZROWS = SIDE // ZCH
PCH = 2
PROWS = TILE // 4 // PCH
FIRST = 10
CX = {4: (0,), 7: (1, 2)}
CY = {8: (0,), 11: (1, 2)}
PC_SLOT = 20
PER_SLOT = 4
VMEM_LIMIT = 40 * 2**20
UPDATE_LIMIT = 24 * 2**20
EXACT = lax.Precision.HIGHEST
MESH = pl.DeviceIdType.MESH


def dot(left, right, dims):
    return lax.dot_general(
        left, right, (dims, ((), ())), precision=EXACT, preferred_element_type=jnp.float32
    )


def panel_dot(left, right, dims):
    def split(value):
        high = value.astype(jnp.bfloat16)
        return high, (value - high.astype(jnp.float32)).astype(jnp.bfloat16)

    def part(a, b):
        return lax.dot_general(a, b, (dims, ((), ())), preferred_element_type=jnp.float32)

    left_high, left_low = split(left)
    right_high, right_low = split(right)
    return part(left_high, right_high) + (part(left_high, right_low) + part(left_low, right_high))


def cholesky_inverse(tile):
    sub = lax.broadcasted_iota(jnp.int32, (8, TILE), 0)
    lane = lax.broadcasted_iota(jnp.int32, (8, TILE), 1)
    count = TILE // 8
    a = [tile[8 * i : 8 * i + 8] for i in range(count)]
    w = [jnp.where(lane == sub + 8 * i, 1.0, 0.0) for i in range(count)]
    for start in range(0, TILE, SUP):
        blocks = list(range(start // 8, (start + SUP) // 8))
        for t in blocks:
            j0 = 8 * t
            rest = [m for m in blocks if m >= t]
            col = {
                m: [jnp.broadcast_to(a[m][:, j0 + q : j0 + q + 1], (8, TILE)) for q in range(8)]
                for m in rest
            }
            scale = jnp.zeros((8, TILE), jnp.float32)
            for p in range(8):
                root = lax.rsqrt(jnp.broadcast_to(col[t][p][p : p + 1], (8, TILE)))
                scale = jnp.where(sub == p, root, scale)
                row_a = jnp.broadcast_to(a[t][p : p + 1], (8, TILE)) * root
                row_w = jnp.broadcast_to(w[t][p : p + 1], (8, TILE)) * root
                piece = {
                    q: jnp.broadcast_to(col[t][q][p : p + 1], (8, TILE)) * root
                    for q in range(p + 1, 8)
                }
                for m in rest:
                    factor = col[m][p] * root
                    for q in range(p + 1, 8):
                        col[m][q] = col[m][q] - factor * piece[q]
                    if m == t:
                        factor = jnp.where(sub > p, factor, 0.0)
                    a[m] = a[m] - factor * row_a
                    w[m] = w[m] - factor * row_w
            a[t] = a[t] * scale
            w[t] = w[t] * scale
            yield
        end = start + SUP
        if end < TILE:
            upper = jnp.concatenate([a[m] for m in blocks], 0)
            both = jnp.concatenate([upper, jnp.concatenate([w[m] for m in blocks], 0)], 1)
            change = dot(upper, both, ((0,), (0,)))
            for m in range(end // 8, count):
                a[m] = a[m] - change[8 * m : 8 * m + 8, :TILE]
                w[m] = w[m] - change[8 * m : 8 * m + 8, TILE:]
            yield
    return jnp.concatenate(w, 0)


def place():
    r = lax.axis_index("row")
    c = lax.axis_index("col")
    return r % RING_X, r // RING_X, c // 2, c % 2


def device(x, y, z, k):
    return (y * RING_X + x, z * 2 + k)


def wrap(i, n):
    return lax.rem(i + n, n)


TREE = {
    (0, 0): (0,), (1, 0): (0, 1, 3), (2, 0): (0, 3), (1, 1): (0, 1, 2), (1, 3): (2,),
    (2, 1): (0, 1, 4), (2, 3): (0,), (1, 2): (2,),
}
LEVEL = {(0, 0): 0, (1, 0): 1, (2, 0): 2, (1, 1): 2, (1, 3): 2, (2, 1): 3, (2, 3): 3, (1, 2): 3}
STEPS = ((1, 0), (0, 1), (-1, 0), (0, -1))
HOP = 3
WAVE = 9
Z_FAN = {0: (2, 6), 2: (1, 3, 4), 6: (5, 7)}


def panels_kernel(
    a_ref, a_out, pr_ref, pc_hi_ref, pc_lo_ref,
    hr, hc, cn, w_all,
    cn_recv, cn_send, cn_sib, z_recv, z_send, z_sib_recv, z_sib_send, z_own,
    p_recv, p_send, p_own, a_sem,
):
    x, y, z, k = place()
    r = y * RING_X + x
    sibling = device(x, y, z, 1 - k)
    step = 1 - 2 * k
    pos = jnp.where(k == 0, z, wrap(RING_Z - z, RING_Z))
    around = (
        device(wrap(x + 1, RING_X), y, z, k),
        device(x, wrap(y + 1, RING_Y), z, k),
        device(wrap(x - 1, RING_X), y, z, k),
        device(x, wrap(y - 1, RING_Y), z, k),
    )
    corners = tuple(
        device(wrap(x + dx, RING_X), wrap(y + dy, RING_Y), z, k)
        for dx, dy in ((1, 1), (-1, 1), (-1, -1), (1, -1))
    )
    z_next = device(x, y, wrap(z + step, RING_Z), k)
    z_prev = device(x, y, wrap(z - step, RING_Z), k)
    z_skip = device(x, y, wrap(z + 2 * step, RING_Z), k)
    z_back = device(x, y, wrap(z - 2 * step, RING_Z), k)
    x_far = device(wrap(x + 2, RING_X), y, z, k)
    y_far = device(x, wrap(y + 2, RING_Y), z, k)

    pltpu.make_async_copy(a_ref, a_out, a_sem).start()
    barrier = pltpu.get_barrier_semaphore()

    def greet(target):
        pl.semaphore_signal(barrier, inc=1, device_id=target, device_id_type=MESH)

    for target in (sibling, z_next, z_prev, x_far, y_far) + around + corners:
        greet(target)

    @pl.when(pos == 4)
    def _():
        greet(z_back)

    root_core = (0, 0, 1)
    root_x = (0, 1, 1)
    count = 13 + jnp.where(pos == 2, 1, 0)
    for tile in range(3):
        in_ring = jnp.logical_and(jnp.logical_and(x == root_x[tile], y == 0), k == root_core[tile])

        def greet_ring(where_, place_z, tile=tile, in_ring=in_ring):
            @pl.when(jnp.logical_and(in_ring, where_))
            def _():
                greet((root_x[tile], place_z * 2 + root_core[tile]))

        if tile == 0:
            greet_ring(z != 0, 0)
            count = count + jnp.where(jnp.logical_and(in_ring, z == 0), 7, 0)
        else:
            greet_ring(jnp.logical_or(z == 2, z == 6), 0)
            greet_ring(jnp.logical_or(z == 1, jnp.logical_or(z == 3, z == 4)), 2)
            greet_ring(jnp.logical_or(z == 5, z == 7), 6)
            fan = jnp.where(z == 2, 3, jnp.where(jnp.logical_or(z == 0, z == 6), 2, 0))
            count = count + jnp.where(in_ring, fan, 0)

    pl.semaphore_wait(barrier, count)

    def remote(src, dst, send, recv, target):
        return pltpu.make_async_remote_copy(
            src_ref=src, dst_ref=dst, send_sem=send, recv_sem=recv, device_id=target,
            device_id_type=MESH,
        )

    corner_src = a_ref.at[0:TILE, 0:TILE]

    def corner_z(tile):
        mine = jnp.logical_and(jnp.logical_and(x == root_x[tile], y == 0), k == root_core[tile])

        @pl.when(jnp.logical_and(mine, z == 0))
        def _():
            targets = Z_FAN[0] if tile else tuple(range(1, RING_Z))
            for i, to in enumerate(targets):
                remote(
                    corner_src, cn.at[tile], cn_send.at[tile, i],
                    cn_recv.at[tile], (root_x[tile], to * 2 + root_core[tile]),
                ).start()
            pltpu.make_async_copy(corner_src, cn.at[tile], cn_recv.at[tile]).start()

    def corner_wait(tile):
        pltpu.make_async_copy(corner_src, cn.at[tile], cn_recv.at[tile]).wait()

    def corner_send(tile, sem, target):
        remote(cn.at[tile], cn.at[tile], cn_send.at[tile, sem], cn_recv.at[tile], target).start()

    def corner_x(tile):
        mine = jnp.logical_and(jnp.logical_and(x == root_x[tile], y == 0), k == root_core[tile])

        @pl.when(mine)
        def _():
            corner_wait(tile)
            if tile:
                for place_z in (2, 6):

                    @pl.when(z == place_z)
                    def _(place_z=place_z):
                        for i, to in enumerate(Z_FAN[place_z]):
                            corner_send(tile, i, (root_x[tile], to * 2 + root_core[tile]))

            corner_send(tile, 7, around[0])
            corner_send(tile, 8, around[2])
            corner_send(tile, 9, x_far)
            corner_send(tile, 10, around[1])
            corner_send(tile, 11, around[3])
            corner_send(tile, 12, y_far)
            remote(cn.at[tile], cn.at[tile], cn_sib.at[tile], cn_recv.at[tile], sibling).start()

    def corner_y(tile):
        mine = jnp.logical_and(k == root_core[tile], jnp.logical_and(y == 0, x != root_x[tile]))

        @pl.when(mine)
        def _():
            corner_wait(tile)
            corner_send(tile, 10, around[1])
            corner_send(tile, 11, around[3])
            corner_send(tile, 12, y_far)
            remote(cn.at[tile], cn.at[tile], cn_sib.at[tile], cn_recv.at[tile], sibling).start()

    def corner_end(tile):
        @pl.when(jnp.logical_and(k == root_core[tile], y != 0))
        def _():
            corner_wait(tile)
            remote(cn.at[tile], cn.at[tile], cn_sib.at[tile], cn_recv.at[tile], sibling).start()

        @pl.when(k != root_core[tile])
        def _():
            corner_wait(tile)

    def corner_drain(tile):
        mine = k == root_core[tile]
        here = cn.at[tile]

        def sent(sem):
            remote(here, here, sem, cn_recv.at[tile], sibling).wait_send()

        @pl.when(mine)
        def _():
            sent(cn_sib.at[tile])

            @pl.when(y == 0)
            def _():
                for i in (10, 11, 12):
                    sent(cn_send.at[tile, i])

            @pl.when(jnp.logical_and(y == 0, x == root_x[tile]))
            def _():
                for i in (7, 8, 9):
                    sent(cn_send.at[tile, i])

                for place_z in (0, 2, 6) if tile else (0,):

                    @pl.when(z == place_z)
                    def _(place_z=place_z):
                        for i in range(len(Z_FAN[place_z]) if tile else 7):
                            sent(cn_send.at[tile, i])

    def z_rows(j):
        return pl.ds(j * ZROWS, ZROWS)

    def z_send_chunk(j, way, src, target):
        remote(src, hr.at[k, z_rows(j)], z_send.at[way], z_recv.at[j], target).start()

    def z_sibling(j, src):
        remote(src, hr.at[k, z_rows(j)], z_sib_send, z_sib_recv.at[j], sibling).start()

    def z_service(j, place_here):
        @pl.when(pos == place_here)
        def _():
            here = hr.at[k, z_rows(j)]
            pltpu.make_async_copy(here, here, z_recv.at[j]).wait()
            if place_here in (1, 2, 4):
                z_send_chunk(j, 0, here, z_next)
            if place_here == 2:
                z_send_chunk(j, 1, here, z_skip)
            if place_here == 7:
                z_send_chunk(j, 0, here, z_prev)
            z_sibling(j, here)

    whole_r = hr.at[k]

    def z_sent(way):
        remote(whole_r, whole_r, z_send.at[way], z_sib_recv.at[0], sibling).wait_send()

    trees = []
    for s in range(2):
        for d in range(4):
            fx, fy = wrap(x - s + RING_X, RING_X), y
            for _ in range(d):
                fx, fy = fy, wrap(RING_X - fx, RING_X)
            at = fx + RING_X * fy
            trees.append((s, d, at))

    def p_rows(d, j):
        start = d * (TILE // 4) + j * PROWS
        return slice(start, start + PROWS)

    def among(at, spots):
        found = at == spots[0][0] + RING_X * spots[0][1]
        for spot in spots[1:]:
            found = jnp.logical_or(found, at == spot[0] + RING_X * spot[1])
        return found

    def p_service(index, j, level):
        s, d, at = trees[index]
        here = hc.at[s, p_rows(d, j)]
        spots = [spot for spot in TREE if LEVEL[spot] == level]

        @pl.when(among(at, spots))
        def _():
            if level == 0:
                src = a_ref.at[p_rows(d, j)]
            else:
                src = here
                pltpu.make_async_copy(here, here, p_recv.at[index, j]).wait()
            for way in range(5):
                users = [spot for spot in spots if way in TREE[spot]]
                if users:

                    def send(way=way):
                        remote(
                            src, here, p_send.at[index, way], p_recv.at[index, j],
                            corners[d] if way == 4 else around[(way + d) % 4],
                        ).start()

                    if len(users) == len(spots):
                        send()
                    else:
                        pl.when(among(at, users))(send)

    def p_end(index):
        s, d, at = trees[index]

        @pl.when(jnp.logical_not(among(at, list(TREE))))
        def _():
            for j in range(PCH):
                here = hc.at[s, p_rows(d, j)]
                pltpu.make_async_copy(here, here, p_recv.at[index, j]).wait()

    def p_drain(index):
        s, d, at = trees[index]
        part = hc.at[s, d * (TILE // 4) : (d + 1) * (TILE // 4)]

        @pl.when(among(at, list(TREE)))
        def _():
            for way in range(5):

                @pl.when(among(at, [spot for spot in TREE if way in TREE[spot]]))
                def _(way=way):
                    remote(
                        part, part, p_send.at[index, way], p_recv.at[index, 0], sibling
                    ).wait_send()

    for tile in range(3):
        corner_z(tile)

    @pl.when(pos == 0)
    def _():
        for j in range(ZCH):
            z_send_chunk(j, 0, a_ref.at[z_rows(j), 0:TILE], z_next)
        for j in range(ZCH):
            z_sibling(j, a_ref.at[z_rows(j), 0:TILE])
        pltpu.make_async_copy(a_ref.at[:, 0:TILE], hr.at[k], z_own).start()

    for j in range(PCH):
        for index in range(8):
            p_service(index, j, 0)

    @pl.when(r < 2)
    def _():
        pltpu.make_async_copy(a_ref.at[0:TILE, :], hc.at[r], p_own).start()

    def second_wave():
        @pl.when(pos == 0)
        def _():
            z_sent(0)
            for j in range(ZCH):
                z_send_chunk(j, 1, a_ref.at[z_rows(j), 0:TILE], z_prev)

    z_level = {1: 0, 2: 1, 3: 2, 4: 2, 5: 3, 7: 3, 6: 4}
    def slot_work(slot):
        if slot in CX:
            for tile in CX[slot]:
                corner_x(tile)
        if slot == WAVE:
            second_wave()
        if slot in CY:
            for tile in CY[slot]:
                corner_y(tile)
        for j in range(ZCH):
            for where_, level in ((1, 1), (2, 2), (3, 3), (4, 3), (5, 4)):
                if HOP * level + j * 8 // ZCH == slot:
                    z_service(j, where_)
            for where_, level in ((7, 1), (6, 2)):
                if WAVE + 1 + HOP * level + j * 8 // ZCH == slot:
                    z_service(j, where_)
        for j in range(PCH):
            for level in range(1, 4):
                if HOP * level + 2 * j == slot:
                    for index in range(8):
                        p_service(index, j, level)

    def chain():
        corner_end(0)
        w0 = yield from cholesky_inverse(cn[0])
        w_all[:TILE, :TILE] = w0
        w_all[:TILE, TILE:] = jnp.zeros((TILE, TILE), jnp.float32)
        corner_end(1)
        corner_end(2)
        u01 = dot(w0, cn[1], ((1,), (1,)))
        w_all[TILE:, :TILE] = dot(u01, w0, ((0,), (0,)))
        yield
        w1 = yield from cholesky_inverse(cn[2] - dot(u01, u01, ((0,), (0,))))
        w_all[TILE:, TILE:] = w1
        w_all[TILE:, :TILE] = -dot(w1, w_all[TILE:, :TILE], ((1,), (0,)))

    def columns():
        @pl.when(r < 2)
        def _():
            pltpu.make_async_copy(a_ref.at[0:TILE, :], hc.at[r], p_own).wait()

        for index in range(8):
            p_end(index)
        for i in range(SIDE // 256):
            lanes = slice(i * 256, i * 256 + 256)
            raw = jnp.concatenate([hc[0, :, lanes], hc[1, :, lanes]], axis=0)
            got = panel_dot(w_all[...], raw, ((1,), (0,)))
            high = got.astype(jnp.bfloat16)
            pc_hi_ref[:, lanes] = high
            pc_lo_ref[:, lanes] = (got - high.astype(jnp.float32)).astype(jnp.bfloat16)

        @pl.when(pos == 0)
        def _():
            pltpu.make_async_copy(a_ref.at[:, 0:TILE], hr.at[k], z_own).wait()

        pltpu.make_async_copy(a_ref, a_out, a_sem).wait()

    def rows_done():
        for j in range(ZCH):
            other = hr.at[1 - k, z_rows(j)]
            pltpu.make_async_copy(other, other, z_sib_recv.at[j]).wait()
        for i in range(SIDE // 256):
            rows = slice(i * 256, i * 256 + 256)
            raw = jnp.concatenate([hr[0, rows], hr[1, rows]], axis=1)
            pr_ref[rows] = panel_dot(raw, w_all[...], ((1,), (1,)))

    def work():
        yield from chain()
        yield
        while len(slots_seen) < PC_SLOT:
            yield
        columns()
        yield
        while len(slots_seen) < 50:
            yield
        for tile in range(3):
            corner_drain(tile)
        for index in range(8):
            p_drain(index)
        rows_done()

    slots_seen = []
    steps = work()
    for slot in range(1, WAVE + 16):
        slots_seen.append(slot)
        slot_work(slot)
        if slot >= FIRST:
            for _ in range(PER_SLOT):
                next(steps, None)
    slots_seen.extend(range(100))
    for _ in steps:
        pass

    remote(whole_r, whole_r, z_sib_send, z_sib_recv.at[0], sibling).wait_send()

    @pl.when(jnp.logical_or(jnp.logical_or(pos == 1, pos == 2), jnp.logical_or(pos == 4, pos == 7)))
    def _():
        z_sent(0)

    @pl.when(jnp.logical_or(pos == 0, pos == 2))
    def _():
        z_sent(1)


def panels(matrix):
    vmem = pl.BlockSpec(memory_space=pltpu.VMEM)
    f32 = jnp.float32
    dma = pltpu.SemaphoreType.DMA
    return pl.pallas_call(
        panels_kernel,
        out_shape=[
            pltpu.VMEM((SIDE, SIDE), f32),
            pltpu.VMEM((SIDE, 2 * TILE), f32),
            pltpu.VMEM((2 * TILE, SIDE), jnp.bfloat16),
            pltpu.VMEM((2 * TILE, SIDE), jnp.bfloat16),
        ],
        in_specs=[pl.BlockSpec(memory_space=pl.ANY)],
        out_specs=[vmem] * 4,
        scratch_shapes=[
            pltpu.VMEM((2, SIDE, TILE), f32),
            pltpu.VMEM((2, TILE, SIDE), f32),
            pltpu.VMEM((3, TILE, TILE), f32),
            pltpu.VMEM((2 * TILE, 2 * TILE), f32),
            dma((3,)), dma((3, 13)), dma((3,)),
            dma((ZCH,)), dma((2,)), dma((ZCH,)), dma, dma,
            dma((8, PCH)), dma((8, 5)), dma, dma,
        ],
        compiler_params=pltpu.CompilerParams(
            collective_id=0, has_side_effects=True, vmem_limit_bytes=VMEM_LIMIT
        ),
        name="panels",
    )(matrix)


def finished(i, raw, panel, pc_hi_ref, pc_lo_ref):
    r = lax.axis_index("row")
    c = lax.axis_index("col")

    def part(left, right):
        return lax.dot_general(
            left, right[...], (((1,), (0,)), ((), ())), preferred_element_type=jnp.float32
        )

    high = panel.astype(jnp.bfloat16)
    low = (panel - high.astype(jnp.float32)).astype(jnp.bfloat16)
    full = raw - (part(high, pc_hi_ref) + (part(high, pc_lo_ref) + part(low, pc_hi_ref)))
    first = jnp.where(c == 0, panel[:, :TILE], jnp.where(c == 1, panel[:, TILE:], full[:, :TILE]))
    wide = full[:, TILE:]
    if i == 0:
        row = lax.broadcasted_iota(jnp.int32, (TILE, TILE), 0)
        lane = lax.broadcasted_iota(jnp.int32, (TILE, TILE), 1)
        kept = jnp.logical_or(c < r, jnp.logical_and(c == r, lane <= row))
        first = jnp.where(jnp.logical_and(r < 2, jnp.logical_not(kept)), 0.0, first)
        wide = jnp.where(r < 2, 0.0, wide)
    return first, wide


def finish_kernel(a_ref, pr_ref, pc_hi_ref, pc_lo_ref, out_ref, stage, sem):
    copies = []
    for i in range(SIDE // TILE):
        rows = slice(i * TILE, (i + 1) * TILE)
        first, wide = finished(i, a_ref[rows], pr_ref[rows], pc_hi_ref, pc_lo_ref)
        stage[rows, :TILE] = first
        stage[rows, TILE:] = wide
        copies.append(pltpu.make_async_copy(stage.at[rows], out_ref.at[rows], sem.at[i]))
        copies[-1].start()
    for copy in copies:
        copy.wait()


def finish(a, pr, pc_hi, pc_lo):
    vmem = pl.BlockSpec(memory_space=pltpu.VMEM)
    return pl.pallas_call(
        finish_kernel,
        out_shape=jax.ShapeDtypeStruct((SIDE, SIDE), jnp.float32),
        in_specs=[vmem] * 4,
        out_specs=pl.BlockSpec(memory_space=pl.ANY),
        scratch_shapes=[
            pltpu.VMEM((SIDE, SIDE), jnp.float32), pltpu.SemaphoreType.DMA((SIDE // TILE,)),
        ],
        compiler_params=pltpu.CompilerParams(vmem_limit_bytes=UPDATE_LIMIT),
        name="finish",
    )(a, pr, pc_hi, pc_lo)


def per_device(matrix):
    return finish(*panels(matrix))


def solution(mesh):
    return jax.shard_map(
        per_device, mesh=mesh, in_specs=(P("row", "col"),), out_specs=P("row", "col"),
        check_vma=False,
    )
```
